32 devices in a mesh: sub: 8 (over z, core), mem: 4 (over y, x).
Axes of the slice: x: 2, y: 2, z: 4, core: 2. Of those that a mesh axis runs over, the one named last changes fastest.
Arguments:
- dechirped_echo_matrix: bfloat16 [8, 2, 256, 8192], P('sub', None, 'mem'), may hold values from -6 to 6
- bearing_rotation_table: float32 [8, 4, 512, 256], P('sub', 'mem'), may hold values from -3.140625 to 3.140625
- patch_subset_holder: int32 [8, 4, 64], P('sub', 'mem'), may hold values from 0 to 7, as said below
- modulation_slope: float32 [8, 4, 2, 64], P('sub', 'mem'), may hold values from -0.5 to 0.5
- regrid_lead_cell: int32 [8, 4, 2, 128], P('sub', 'mem'), may hold values from 0 to 124
- regrid_weight: float32 [8, 4, 2, 128], P('sub', 'mem'), may hold values from 0 to 1
Outputs:
- ground_image: bfloat16 [32, 2, 128, 128], P(('sub', 'mem'))
The draws below stay inside these ranges and needn't reach their ends.
Inputs may be any that keep to these rules, and one draw needn't show every extreme that they name: `patch_subset_holder`: each group and sector sends at most 16 of its 64 blocks to any one tile; in every sector some tile receives exactly 16 blocks from every group.
All inputs are finite; a program needn't handle non-finite values.
Results may differ from the reference program's by a relative error of at most 0.014.
Values may be sent and summed in bfloat16 or wider, within the bound.
A program may use at most 64 MiB of HBM per device.

```python
import math
import jax
import jax.numpy as jnp
from jax import lax

FREQUENCIES = 8192
FIRST_RADIX = 64
SECOND_RADIX = 128
SWEEPS = 256
ANGLES = 512
BLOCK_SIDE = 128
LOOK_SUBSETS = 8
SLANT_DIVISIONS = 4
SECTOR_BINS = 2048
TILT_PATCH_COUNT = 4
SLANT_PATCHES = 16
PATCHES_IN_SLICE = 64
CAPACITY = 16
TILES = 32


def draw_patch_subset_holder(key, part):
    full_key = jax.random.fold_in(key, 11)
    fullest = jax.random.randint(full_key, (SLANT_DIVISIONS,), 0, LOOK_SUBSETS, dtype=jnp.int32)
    targets = jnp.tile(fullest, LOOK_SUBSETS)
    numbers = jnp.arange(LOOK_SUBSETS * SLANT_DIVISIONS, dtype=jnp.int32) + 100
    seed_keys = jax.vmap(lambda number: jax.random.fold_in(key, number))(numbers)

    def one_device(seed_key, target):
        order_key = jax.random.fold_in(seed_key, 1)
        place_key = jax.random.fold_in(seed_key, 2)
        others = jnp.arange(LOOK_SUBSETS - 1, dtype=jnp.int32)
        others = others + (others >= target).astype(jnp.int32)
        pool_list = jnp.repeat(others, CAPACITY)
        pool_list = jax.random.permutation(order_key, pool_list)
        chosen = jnp.concatenate([jnp.full((CAPACITY,), target, dtype=jnp.int32), pool_list[:PATCHES_IN_SLICE - CAPACITY]])
        return jax.random.permutation(place_key, chosen)
    owners = jax.vmap(one_device)(seed_keys, targets)
    return owners.reshape(LOOK_SUBSETS, SLANT_DIVISIONS, PATCHES_IN_SLICE).astype(jnp.int32)


def plant(drawn, stream_key, smallest, top_value):
    place = [jax.random.randint(jax.random.fold_in(stream_key, axis), (), 0, length) for axis, length in enumerate(drawn.shape)]
    longest = drawn.shape.index(max(drawn.shape))
    neighbour = place[:longest] + [(place[longest] + 1) % drawn.shape[longest]] + place[longest + 1:]
    return drawn.at[tuple(place)].set(smallest).at[tuple(neighbour)].set(top_value)


def block_scale(rng, dims, split, least, top_value):
    def one(position, parts):
        draws = jax.random.uniform(jax.random.fold_in(jax.random.fold_in(rng, 6), position), (parts,), jnp.float32, least / len(split), top_value / len(split))
        return jnp.repeat(jnp.exp(draws), dims[position] // parts).reshape((-1,) + (1,) * (len(dims) - position - 1))

    gain = one(*split[0])
    for cut in split[1:]:
        gain = gain * one(*cut)
    return gain


def bell_draw(stream_key, dims, width, most, pieces=(), kind=jnp.bfloat16):
    factor_of = block_scale(stream_key, dims, pieces, -0.22, 0.18) if pieces else 1.0
    result = jax.random.normal(stream_key, dims, jnp.float32) * width * factor_of
    return jnp.minimum(jnp.maximum(result, -most), most).astype(kind)


def setup_inputs(seed: int = 0) -> dict:
    key_list = jax.random.split(jax.random.key(seed), 7)
    dechirped_echo_matrix = bell_draw(key_list[0], (LOOK_SUBSETS, 2, SWEEPS, FREQUENCIES), 1.0, 6.0, ((0, 8), (2, 4)))
    bearing_rotation_table = jnp.clip(jax.random.uniform(key_list[1], (LOOK_SUBSETS, SLANT_DIVISIONS, ANGLES, SWEEPS), jnp.float32, -3.140625, 3.140625), -3.140625, 3.140625)
    patch_subset_holder = draw_patch_subset_holder(jax.random.fold_in(key_list[6], 71), 0)
    modulation_slope = jnp.clip(jax.random.uniform(key_list[3], (LOOK_SUBSETS, SLANT_DIVISIONS, 2, PATCHES_IN_SLICE), jnp.float32, -0.5, 0.5) * block_scale(key_list[3], (LOOK_SUBSETS, SLANT_DIVISIONS, 2, PATCHES_IN_SLICE), ((0, 8), (1, 4)), -0.4, 0.0), -0.5, 0.5)
    regrid_lead_cell = plant(jax.random.randint(key_list[4], (LOOK_SUBSETS, SLANT_DIVISIONS, 2, BLOCK_SIDE), 0, BLOCK_SIDE - 3), jax.random.fold_in(key_list[4], 1), 0, (BLOCK_SIDE - 3) - 1).astype(jnp.int32)
    regrid_weight = jnp.clip(1.0 * jax.random.uniform(key_list[5], (LOOK_SUBSETS, SLANT_DIVISIONS, 2, BLOCK_SIDE), jnp.float32) ** block_scale(key_list[5], (LOOK_SUBSETS, SLANT_DIVISIONS, 2, BLOCK_SIDE), ((0, 8), (1, 4)), -0.2, 0.2), 0.0, 1.0)
    return dict(dechirped_echo_matrix=dechirped_echo_matrix, bearing_rotation_table=bearing_rotation_table, patch_subset_holder=patch_subset_holder, modulation_slope=modulation_slope, regrid_lead_cell=regrid_lead_cell, regrid_weight=regrid_weight)


def dft_tables(length):
    positions = jnp.arange(length, dtype=jnp.int32)
    turns = positions[:, None] * positions[None, :] % length
    phase_angle = turns.astype(jnp.float32) * (2.0 * math.pi / length)
    return jnp.stack([jnp.cos(phase_angle), jnp.sin(phase_angle)]).astype(jnp.bfloat16)

def twiddle(row_count, column_count, length):
    row_index = jnp.arange(row_count, dtype=jnp.int32)
    column_index = jnp.arange(column_count, dtype=jnp.int32)
    turns = row_index[:, None] * column_index[None, :] % length
    phase_angle = turns.astype(jnp.float32) * (2.0 * math.pi / length)
    return (jnp.cos(phase_angle), jnp.sin(phase_angle))

def combine(product):
    return (product[0, 0] - product[1, 1], product[0, 1] + product[1, 0])

def range_transform(sweeps):
    sweep_count = sweeps.shape[1]
    reshaped = sweeps.reshape(2, sweep_count, FIRST_RADIX, SECOND_RADIX).astype(jnp.float32)
    product = jnp.einsum('qrk,pskj->qpsrj', dft_tables(FIRST_RADIX).astype(jnp.float32), reshaped)
    inphase_part, quadrature_part = combine(product)
    cosine, sine_part = twiddle(FIRST_RADIX, SECOND_RADIX, FREQUENCIES)
    turned = jnp.stack([inphase_part * cosine - quadrature_part * sine_part, inphase_part * sine_part + quadrature_part * cosine]).astype(jnp.bfloat16)
    product = jnp.einsum('quj,psrj->qpsur', dft_tables(SECOND_RADIX).astype(jnp.float32), turned.astype(jnp.float32))
    inphase_part, quadrature_part = combine(product)
    factor = 1.0 / math.sqrt(FREQUENCIES)
    return (jnp.stack([inphase_part, quadrature_part]) * factor).astype(jnp.bfloat16).reshape(2, sweep_count, FREQUENCIES)

def phase_tables(angles):
    factor = 1.0 / math.sqrt(SWEEPS)
    return jnp.stack([jnp.cos(angles) * factor, jnp.sin(angles) * factor]).astype(jnp.bfloat16)

def strip_modulation(inphase_part, quadrature_part, modulation_line_entries):
    tilt_linear_slope = modulation_line_entries[0].reshape(TILT_PATCH_COUNT, SLANT_PATCHES)
    slant_linear_slope = modulation_line_entries[1].reshape(TILT_PATCH_COUNT, SLANT_PATCHES)
    positions = jnp.arange(BLOCK_SIDE, dtype=jnp.float32)
    phase_angle = tilt_linear_slope[:, None, :, None] * positions[None, :, None, None] + slant_linear_slope[:, None, :, None] * positions[None, None, None, :]
    cosine = jnp.cos(phase_angle)
    sine_part = jnp.sin(phase_angle)
    inphase_part = inphase_part.reshape(TILT_PATCH_COUNT, BLOCK_SIDE, SLANT_PATCHES, BLOCK_SIDE)
    quadrature_part = quadrature_part.reshape(TILT_PATCH_COUNT, BLOCK_SIDE, SLANT_PATCHES, BLOCK_SIDE)
    return jnp.stack([inphase_part * cosine - quadrature_part * sine_part, inphase_part * sine_part + quadrature_part * cosine]).astype(jnp.bfloat16)

def stencil(offsets, fractions):
    shift_part = fractions
    weights = [-shift_part * (shift_part - 1.0) * (shift_part - 2.0) / 6.0, (shift_part + 1.0) * (shift_part - 1.0) * (shift_part - 2.0) / 2.0, -(shift_part + 1.0) * shift_part * (shift_part - 2.0) / 2.0, (shift_part + 1.0) * shift_part * (shift_part - 1.0) / 6.0]
    sources = jnp.arange(fractions.shape[-1], dtype=jnp.int32)
    distance = sources - offsets[..., None]
    weights_sum = jnp.zeros(distance.shape, jnp.float32)
    for stencil_tap in range(4):
        weights_sum = weights_sum + jnp.where(distance == stencil_tap, weights[stencil_tap][..., None], jnp.float32(0.0))
    return weights_sum.astype(jnp.bfloat16)

def reference(dechirped_echo_matrix, bearing_rotation_table, patch_subset_holder, modulation_slope, regrid_lead_cell, regrid_weight):
    tables_all = stencil(regrid_lead_cell, regrid_weight).reshape(TILES, 2, BLOCK_SIDE, BLOCK_SIDE)
    sector_rows = jnp.arange(SLANT_DIVISIONS, dtype=jnp.int32)

    def lone_subset(picture_buffer, inputs):
        history, angles, owners, linear_slopes = inputs
        spectrum = range_transform(history)
        by_sector = spectrum.reshape(2, SWEEPS, SLANT_DIVISIONS, SECTOR_BINS).astype(jnp.float32)
        product = jnp.einsum('qmas,psmc->qpmac', phase_tables(angles).astype(jnp.float32), by_sector)
        inphase_part, quadrature_part = combine(product)
        patch_list = jax.vmap(strip_modulation)(inphase_part, quadrature_part, linear_slopes)
        tile_index = (owners * SLANT_DIVISIONS + sector_rows[:, None]).astype(jnp.int32)
        chosen = tables_all[tile_index.reshape(-1)].reshape(SLANT_DIVISIONS, TILT_PATCH_COUNT, SLANT_PATCHES, 2, BLOCK_SIDE, BLOCK_SIDE).astype(jnp.float32)
        rows_done = jnp.einsum('mACya,mpAaCc->mACpyc', chosen[:, :, :, 0], patch_list.astype(jnp.float32)).astype(jnp.bfloat16)
        interpolated = jnp.einsum('mACpyc,mACxc->mACpyx', rows_done.astype(jnp.float32), chosen[:, :, :, 1])
        partial_sum = jax.ops.segment_sum(interpolated.reshape(-1, 2, BLOCK_SIDE, BLOCK_SIDE), tile_index.reshape(-1), num_segments=TILES)
        rounded = lax.optimization_barrier(partial_sum.astype(jnp.bfloat16)).astype(jnp.float32)
        return (picture_buffer + rounded, None)
    initial_location = jnp.zeros((TILES, 2, BLOCK_SIDE, BLOCK_SIDE), jnp.float32)
    picture_buffer, discarded_entry = lax.scan(lone_subset, initial_location, (dechirped_echo_matrix, bearing_rotation_table, patch_subset_holder, modulation_slope))
    return (0.25 * picture_buffer).astype(jnp.bfloat16)
```

```python
import functools
import math

import jax
import jax.numpy as jnp
import ml_dtypes
import numpy as np
from jax import lax
from jax.experimental import pallas as pl
from jax.experimental.pallas import tpu as pltpu
from jax.sharding import PartitionSpec as P

SIDE = 128
F32 = jnp.float32
BF16 = jnp.bfloat16
VMEM_LIMIT = 48 * 1024 * 1024


def transform_tables(frequencies):
    coarse = frequencies // SIDE
    k2 = np.arange(coarse)
    k1 = np.arange(SIDE)
    first = 2.0 * np.pi * ((k2[:, None] * k2[None, :]) % coarse) / coarse
    second = 2.0 * np.pi * ((k2[:, None] * k1[None, :]) % coarse) / coarse
    turn = 2.0 * np.pi * (k1[:, None] * k1[None, :]) / frequencies

    def block(angle):
        c, s = np.cos(angle), np.sin(angle)
        return np.block([[c, -s], [s, c]]).astype(ml_dtypes.bfloat16)

    scale = 1.0 / math.sqrt(frequencies)
    turning = np.stack([np.cos(turn), np.sin(turn)]) * scale
    return block(first), block(second), turning.astype(np.float32)


def cos_sin(x):
    q = jnp.floor(x * (2.0 / math.pi) + 0.5)
    r = x - q * 1.5703125
    r = r - q * 4.837512969970703e-4
    r = r - q * 7.549789948768648e-8
    z = r * r
    s = r + r * z * (-1.6666654611e-1 + z * (8.3321608736e-3 + z * -1.9515295891e-4))
    c = 1.0 - 0.5 * z + z * z * (4.166664568298827e-2 + z * (-1.388731625493765e-3 + z * 2.443315711809948e-5))
    n = q.astype(jnp.int32)
    odd = (n & 1) == 1
    cos_base = jnp.where(odd, s, c)
    sin_base = jnp.where(odd, c, s)
    cos_neg = ((n + 1) & 2) == 2
    sin_neg = (n & 2) == 2
    return jnp.where(cos_neg, -cos_base, cos_base), jnp.where(sin_neg, -sin_base, sin_base)


def transform_kernel(x_ref, w1_ref, w2_ref, turn_ref, out_ref, xs, ys):
    sweeps = x_ref.shape[1]
    coarse = x_ref.shape[2] // SIDE
    members = out_ref.shape[0]
    bands = out_ref.shape[2]

    def spread(k2, carry):
        lanes = pl.ds(pl.multiple_of(k2 * SIDE, SIDE), SIDE)
        for p in range(2):
            rows = pl.ds(pl.multiple_of((p * coarse + k2) * sweeps, 16), sweeps)
            xs[rows, :] = x_ref[p, :, lanes].astype(F32)
        return carry

    lax.fori_loop(0, coarse, spread, 0, unroll=8)

    batch = 8

    def transform(step, carry):
        w1 = w1_ref[...]
        w2 = w2_ref[...]
        for j in range(batch):
            s = step * batch + j
            x = xs[pl.ds(s, 2 * coarse, stride=sweeps), :].astype(BF16)
            f = jnp.dot(w1, x, preferred_element_type=F32)
            re = jnp.concatenate([f[:coarse], f[:coarse]], axis=0)
            im = jnp.concatenate([f[coarse:], f[coarse:]], axis=0)
            cosine, sine = turn_ref[0], turn_ref[1]
            turned = jnp.concatenate(
                [(re * cosine - im * sine).astype(BF16), (re * sine + im * cosine).astype(BF16)], axis=1
            )
            y = lax.dot_general(w2, turned, (((1,), (1,)), ((), ())), preferred_element_type=F32)
            ys[pl.ds(s, 2 * coarse, stride=sweeps), :] = y
        return carry

    lax.fori_loop(0, sweeps // batch, transform, 0)

    def gather(band, carry):
        for m in range(members):
            for p in range(2):
                row = (p * coarse + m * bands + band) * sweeps
                out_ref[m, p, band] = ys[pl.ds(pl.multiple_of(row, 16), sweeps), :].astype(BF16)
        return carry

    lax.fori_loop(0, bands, gather, 0, unroll=2)


def range_transform(x, members):
    _, sweeps, frequencies = x.shape
    coarse = frequencies // SIDE
    w1, w2, turning = transform_tables(frequencies)
    return pl.pallas_call(
        transform_kernel,
        out_shape=jax.ShapeDtypeStruct((members, 2, coarse // members, sweeps, SIDE), BF16),
        in_specs=[pl.BlockSpec(memory_space=pltpu.VMEM)] * 4,
        out_specs=pl.BlockSpec(memory_space=pltpu.VMEM),
        scratch_shapes=[
            pltpu.VMEM((2 * coarse * sweeps, SIDE), F32),
            pltpu.VMEM((2 * coarse * sweeps, SIDE), F32),
        ],
        compiler_params=pltpu.CompilerParams(vmem_limit_bytes=VMEM_LIMIT),
    )(x, jnp.asarray(w1), jnp.asarray(w2), jnp.asarray(turning))


def image_kernel(
    owners_ref, spec_ref, angle_ref, tilt_ref, slant_ref, lead_ref, weight_ref, out_ref,
    lhs, stencils, acc, tilt_tab, slant_tab,
):
    members, _, bands, sweeps, _ = spec_ref.shape
    angles, all_sweeps = angle_ref.shape
    groups = out_ref.shape[0]
    tilts = angles // SIDE
    factor = 1.0 / math.sqrt(all_sweeps)

    for a in range(0, angles, SIDE):
        rows = slice(a, a + SIDE)
        c, s = cos_sin(angle_ref[rows, :])
        c, s = c * factor, s * factor
        lhs[rows, :all_sweeps] = c.astype(BF16)
        lhs[rows, all_sweeps:] = (-s).astype(BF16)
        low = slice(angles + a, angles + a + SIDE)
        lhs[low, :all_sweeps] = s.astype(BF16)
        lhs[low, all_sweeps:] = c.astype(BF16)

    along = lax.broadcasted_iota(jnp.int32, (SIDE, SIDE), 0).astype(F32)
    c, s = cos_sin(along * tilt_ref[...])
    tilt_tab[0] = c
    tilt_tab[1] = s
    across = lax.broadcasted_iota(jnp.int32, (slant_ref.shape[0], SIDE), 1).astype(F32)
    c, s = cos_sin(across * slant_ref[...])
    slant_tab[0] = c
    slant_tab[1] = s

    f = weight_ref[...]
    taps = [
        -f * (f - 1.0) * (f - 2.0) / 6.0,
        (f + 1.0) * (f - 1.0) * (f - 2.0) / 2.0,
        -(f + 1.0) * f * (f - 2.0) / 2.0,
        (f + 1.0) * f * (f - 1.0) / 6.0,
    ]
    lead = lead_ref[...]
    cells = lax.broadcasted_iota(jnp.int32, (SIDE, SIDE), 1)
    for g in range(groups):
        for d in range(2):
            column = slice(g * 2 + d, g * 2 + d + 1)
            distance = cells - lead[:, column]
            total = jnp.zeros((SIDE, SIDE), F32)
            for q in range(4):
                total = total + jnp.where(distance == q, taps[q][:, column], 0.0)
            stencils[g, d] = total.astype(BF16)

    acc[...] = jnp.zeros_like(acc)
    pair = 2

    def step(i, carry):
        rhs = []
        for p in range(2):
            for m in range(members):
                rhs.append(jnp.concatenate([spec_ref[m, p, i * pair + j] for j in range(pair)], axis=1))
        rhs = jnp.concatenate(rhs, axis=0)
        shift = lax.rem(SIDE - i * pair * tilts, SIDE)
        cu = pltpu.roll(tilt_tab[0], shift, 1)
        su = pltpu.roll(tilt_tab[1], shift, 1)
        for ab in range(tilts):
            rows = slice(ab * SIDE, (ab + 1) * SIDE)
            low = slice(angles + ab * SIDE, angles + (ab + 1) * SIDE)
            re_pair = jnp.dot(lhs[rows, :], rhs, preferred_element_type=F32)
            im_pair = jnp.dot(lhs[low, :], rhs, preferred_element_type=F32)
            for j in range(pair):
                b = ab * bands + i * pair + j
                re = re_pair[:, j * SIDE:(j + 1) * SIDE]
                im = im_pair[:, j * SIDE:(j + 1) * SIDE]
                lane = j * tilts + ab
                cb = cu[:, lane:lane + 1]
                sb = su[:, lane:lane + 1]
                cv = slant_tab[0, pl.ds(b, 1), :]
                sv = slant_tab[1, pl.ds(b, 1), :]
                cosine = cb * cv - sb * sv
                sine = sb * cv + cb * sv
                demod = jnp.concatenate(
                    [(re * cosine - im * sine).astype(BF16), (re * sine + im * cosine).astype(BF16)], axis=1
                )
                owner = owners_ref[b]
                rows_done = jnp.dot(stencils[owner, 0], demod, preferred_element_type=F32).astype(BF16)
                rows_done = jnp.concatenate([rows_done[:, :SIDE], rows_done[:, SIDE:]], axis=0)
                acc[owner] += lax.dot_general(
                    rows_done, stencils[owner, 1], (((1,), (1,)), ((), ())), preferred_element_type=F32
                )
        return carry

    lax.fori_loop(0, bands // pair, step, 0)
    out_ref[...] = acc[...].astype(BF16)


def form_tiles(owners, spec, angles, slopes, lead, weight, groups):
    bands = spec.shape[2]
    tilts = angles.shape[0] // SIDE
    blocks = tilts * bands
    tilt = slopes[0].reshape(tilts, bands).T.reshape(1, blocks)
    tilt = jnp.pad(tilt, ((0, 0), (0, SIDE - blocks)))
    vmem = pl.BlockSpec(memory_space=pltpu.VMEM)
    return pl.pallas_call(
        image_kernel,
        out_shape=jax.ShapeDtypeStruct((groups, 2 * SIDE, SIDE), BF16),
        in_specs=[pl.BlockSpec(memory_space=pltpu.SMEM)] + [vmem] * 6,
        out_specs=vmem,
        scratch_shapes=[
            pltpu.VMEM((2 * angles.shape[0], 2 * angles.shape[1]), BF16),
            pltpu.VMEM((groups, 2, SIDE, SIDE), BF16),
            pltpu.VMEM((groups, 2 * SIDE, SIDE), F32),
            pltpu.VMEM((2, SIDE, SIDE), F32),
            pltpu.VMEM((2, blocks, SIDE), F32),
        ],
        compiler_params=pltpu.CompilerParams(vmem_limit_bytes=VMEM_LIMIT),
    )(owners, spec, angles, tilt, slopes[1][:, None], lead, weight)


def on_device(echo, angles, holder, slopes, lead, weight, *, groups, members):
    packed = jnp.concatenate([lead[0, 0].astype(F32), weight[0, 0]], axis=0)
    gathered = lax.all_gather(packed[None], "sub", axis=0, tiled=True)
    columns = jnp.transpose(gathered, (2, 0, 1))
    all_lead = columns[:, :, :2].reshape(SIDE, 2 * groups).astype(jnp.int32)
    all_weight = columns[:, :, 2:].reshape(SIDE, 2 * groups)
    spec = range_transform(echo[0], members)
    spec = lax.all_to_all(spec, "mem", split_axis=0, concat_axis=0, tiled=True)
    tiles = form_tiles(holder[0, 0], spec, angles[0, 0], slopes[0, 0], all_lead, all_weight, groups)
    parts = lax.all_to_all(tiles, "sub", split_axis=0, concat_axis=0, tiled=True)
    total = 0.25 * jnp.sum(parts.astype(F32), axis=0)
    return total.astype(BF16).reshape(1, 2, SIDE, SIDE)


def solution(mesh):
    return jax.shard_map(
        functools.partial(on_device, groups=mesh.shape["sub"], members=mesh.shape["mem"]),
        mesh=mesh,
        in_specs=(
            P("sub", None, "mem", None),
            P("sub", "mem", None, None),
            P("sub", "mem", None),
            P("sub", "mem", None, None),
            P("sub", "mem", None, None),
            P("sub", "mem", None, None),
        ),
        out_specs=P(("sub", "mem"), None, None, None),
        check_vma=False,
    )
```

```python
import functools
import math

import jax
import jax.numpy as jnp
from jax import lax
from jax.experimental import pallas as pl
from jax.experimental.pallas import tpu as pltpu
from jax.sharding import PartitionSpec as P

SIDE = 128
CHUNK = 16
PIECES = 2
F32 = jnp.float32
BF16 = jnp.bfloat16
I32 = jnp.int32
MESH = pl.DeviceIdType.MESH
VMEM_LIMIT = 56 * 1024 * 1024


def cos_sin(x):
    q = jnp.floor(x * (2.0 / math.pi) + 0.5)
    r = x - q * 1.5703125
    r = r - q * 4.837512969970703e-4
    r = r - q * 7.549789948768648e-8
    z = r * r
    s = r + r * z * (-1.6666654611e-1 + z * (8.3321608736e-3 + z * -1.9515295891e-4))
    c = 1.0 - 0.5 * z + z * z * (4.166664568298827e-2 + z * (-1.388731625493765e-3 + z * 2.443315711809948e-5))
    n = q.astype(jnp.int32)
    odd = (n & 1) == 1
    cos_base = jnp.where(odd, s, c)
    sin_base = jnp.where(odd, c, s)
    cos_neg = ((n + 1) & 2) == 2
    sin_neg = (n & 2) == 2
    return jnp.where(cos_neg, -cos_base, cos_base), jnp.where(sin_neg, -sin_base, sin_base)


def iota(rows, columns, dimension):
    return lax.broadcasted_iota(I32, (rows, columns), dimension)


def stacked_transform(coarse, columns):
    turns = (iota(coarse, columns, 0) * iota(coarse, columns, 1)) & (coarse - 1)
    c, s = cos_sin(turns.astype(F32) * (2.0 * math.pi / coarse))
    top = jnp.concatenate([c, -s], axis=1)
    low = jnp.concatenate([s, c], axis=1)
    return jnp.concatenate([top, low], axis=0).astype(BF16)


def down(row):
    return jnp.transpose(jnp.broadcast_to(row, (SIDE, SIDE)))


def stencil(lead_row, weight_row):
    f = down(weight_row)
    taps = [
        -f * (f - 1.0) * (f - 2.0) / 6.0,
        (f + 1.0) * (f - 1.0) * (f - 2.0) / 2.0,
        -(f + 1.0) * f * (f - 2.0) / 2.0,
        (f + 1.0) * f * (f - 1.0) / 6.0,
    ]
    distance = iota(SIDE, SIDE, 1).astype(F32) - down(lead_row.astype(F32))
    total = jnp.zeros((SIDE, SIDE), F32)
    for q in range(4):
        total = total + jnp.where(distance == q, taps[q], 0.0)
    return total.astype(BF16)


def kernel(
    groups, members,
    chain_ref, x_hbm, angle_hbm, slope_ref, lead_ref, weight_ref, out_ref,
    x, angle, xs, ys, w1s, w2s, turn, send, recv, lhs, polar, sums, tilt_tab, slant_tab, stencils,
    pair_out, pair_in, far_out, far_in, own,
    x_sem, angle_sem, mem_send, mem_recv, pair_send, pair_recv, far_send, far_recv,
):
    layers = groups // 2
    _, sweeps, frequencies = x.shape
    coarse = frequencies // SIDE
    bands = coarse // members
    half = bands // PIECES
    chunks = sweeps // CHUNK
    angles, all_sweeps = angle.shape
    tilts = angles // SIDE
    depth = 2 * members * CHUNK
    sub = lax.axis_index("sub")
    me = lax.axis_index("mem")
    layer, core = sub // 2, sub % 2
    partner = layer * 2 + 1 - core

    barrier = pltpu.get_barrier_semaphore()
    for d in range(1, members):
        pl.semaphore_signal(barrier, inc=1, device_id=(sub, (me + d) % members), device_id_type=MESH)
    pl.semaphore_signal(barrier, inc=1, device_id=(partner, me), device_id_type=MESH)
    for d in range(1, layers):
        other = ((layer + d) % layers) * 2 + core
        pl.semaphore_signal(barrier, inc=1, device_id=(other, me), device_id_type=MESH)

    def x_copy(q):
        rows = pl.ds(pl.multiple_of(q * CHUNK, CHUNK), CHUNK)
        return pltpu.make_async_copy(x_hbm.at[:, rows, :], x.at[:, rows, :], x_sem.at[q])

    for q in range(chunks):
        x_copy(q).start()
    angle_copy = pltpu.make_async_copy(angle_hbm, angle, angle_sem)
    angle_copy.start()

    w1s[...] = stacked_transform(coarse, coarse)
    w2s[...] = stacked_transform(coarse, SIDE)
    c, s = cos_sin((iota(SIDE, SIDE, 0) * iota(SIDE, SIDE, 1)).astype(F32) * (2.0 * math.pi / frequencies))
    turn[0] = c * (1.0 / math.sqrt(frequencies))
    turn[1] = s * (1.0 / math.sqrt(frequencies))

    pl.semaphore_wait(barrier, (members - 1) + 1 + (layers - 1))

    def mem_copy(q, piece, d):
        to = (me + d) % members
        return pltpu.make_async_remote_copy(
            src_ref=send.at[to, q, piece],
            dst_ref=recv.at[me, q, piece],
            send_sem=mem_send.at[d - 1, q, piece],
            recv_sem=mem_recv.at[d - 1, q, piece],
            device_id=(sub, to),
            device_id_type=MESH,
        )

    def transform(q, carry):
        x_copy(q).wait()
        rows = pl.ds(pl.multiple_of(q * CHUNK, CHUNK), CHUNK)

        def spread(k2, inner):
            lanes = pl.ds(pl.multiple_of(k2 * SIDE, SIDE), SIDE)
            for p in range(2):
                at = pl.ds(pl.multiple_of((p * coarse + k2) * CHUNK, CHUNK), CHUNK)
                xs[at, :] = x[p, rows, lanes].astype(F32)
            return inner

        lax.fori_loop(0, coarse, spread, 0, unroll=8)

        batch = 8

        def sweep_batch(step, inner):
            w1 = w1s[...]
            w2 = w2s[...]
            for j in range(batch):
                at = pl.ds(step * batch + j, 2 * coarse, stride=CHUNK)
                f = jnp.dot(w1, xs[at, :].astype(BF16), preferred_element_type=F32)
                re = jnp.concatenate([f[:coarse], f[:coarse]], axis=0)
                im = jnp.concatenate([f[coarse:], f[coarse:]], axis=0)
                cosine, sine = turn[0], turn[1]
                turned = jnp.concatenate(
                    [(re * cosine - im * sine).astype(BF16), (re * sine + im * cosine).astype(BF16)], axis=1
                )
                ys[at, :] = lax.dot_general(w2, turned, (((1,), (1,)), ((), ())), preferred_element_type=F32)
            return inner

        lax.fori_loop(0, CHUNK // batch, sweep_batch, 0)

        def pack(m, inner):
            for piece in range(PIECES):
                for p in range(2):
                    for band in range(half):
                        row = (p * coarse + m * bands + piece * half + band) * CHUNK
                        send[m, q, piece, p, band] = ys[pl.ds(pl.multiple_of(row, CHUNK), CHUNK), :].astype(BF16)
            return inner

        lax.fori_loop(0, members, pack, 0)
        for piece in range(PIECES):
            for d in range(1, members):
                mem_copy(q, piece, d).start()
        return carry

    lax.fori_loop(0, chunks, transform, 0)

    angle_copy.wait()
    factor = 1.0 / math.sqrt(all_sweeps)
    wide = 2 * all_sweeps
    source = iota(wide, wide, 0)
    k = iota(wide, wide, 1)
    q_of, p_of = k // depth, (k // (depth // 2)) % 2
    position = ((k // CHUNK) % members) * sweeps + q_of * CHUNK + k % CHUNK
    cos_at = (source == position).astype(F32)
    sin_at = (source == position + all_sweeps).astype(F32)
    first = p_of == 0
    place_re = jnp.where(first, cos_at, -sin_at).astype(BF16)
    place_im = jnp.where(first, sin_at, cos_at).astype(BF16)
    for a in range(tilts):
        c, s = cos_sin(angle[a * SIDE:(a + 1) * SIDE, :])
        table = jnp.concatenate([(c * factor).astype(BF16), (s * factor).astype(BF16)], axis=1)
        lhs[a, 0] = jnp.dot(table, place_re, preferred_element_type=F32).astype(BF16)
        lhs[a, 1] = jnp.dot(table, place_im, preferred_element_type=F32).astype(BF16)

    blocks = slope_ref.shape[1]
    tilt_tab[...] = jnp.zeros_like(tilt_tab)
    tilt_tab[0, :2, :blocks] = slope_ref[...]
    slopes = tilt_tab[0, :2, :]
    tilt_angles = iota(SIDE, SIDE, 0).astype(F32) * slopes[0:1, :]
    slant_angles = iota(SIDE, SIDE, 1).astype(F32) * down(slopes[1:2, :])
    c, s = cos_sin(tilt_angles)
    tilt_tab[0] = c
    tilt_tab[1] = s
    c, s = cos_sin(slant_angles)
    slant_tab[0] = c
    slant_tab[1] = s
    for d in range(2):
        stencils[d] = stencil(lead_ref[d:d + 1, :], weight_ref[d:d + 1, :])
    sums[0] = jnp.zeros((2 * SIDE, SIDE), F32)

    def keep_own(q, carry):
        recv[me, q] = send[me, q]
        return carry

    lax.fori_loop(0, chunks, keep_own, 0)

    def columns(piece, i, q):
        return jnp.concatenate(
            [
                jnp.concatenate([recv[m, q, piece, p, i * 2 + j] for j in range(2)], axis=1)
                for p in range(2)
                for m in range(members)
            ],
            axis=0,
        )

    early = (chunks - 1) * depth
    if chunks > 1:
        def early_wait(q, carry):
            for piece in range(PIECES):
                for d in range(1, members):
                    mem_copy(q, piece, d).wait_recv()
            return carry

        lax.fori_loop(0, chunks - 1, early_wait, 0)
        for piece in range(PIECES):
            def early_step(i, carry, piece=piece):
                rhs = jnp.concatenate([columns(piece, i, q) for q in range(chunks - 1)], axis=0)
                for a in range(tilts):
                    for r in range(2):
                        polar[piece * (half // 2) + i, a, r] = jnp.dot(
                            lhs[a, r, :, :early], rhs, preferred_element_type=F32
                        )
                return carry

            lax.fori_loop(0, half // 2, early_step, 0)

    for piece in range(PIECES):
        for d in range(1, members):
            mem_copy(chunks - 1, piece, d).wait_recv()

        def late_step(i, carry, piece=piece):
            rhs = columns(piece, i, chunks - 1)
            band = piece * half + i * 2
            shift = (SIDE - band) % SIDE
            cu = pltpu.roll(tilt_tab[0], shift, 1)
            su = pltpu.roll(tilt_tab[1], shift, 1)
            for a in range(tilts):
                parts = []
                for r in range(2):
                    part = jnp.dot(lhs[a, r, :, early:], rhs, preferred_element_type=F32)
                    if chunks > 1:
                        part = part + polar[piece * (half // 2) + i, a, r]
                    parts.append(part)
                for j in range(2):
                    b = a * bands + band + j
                    re = parts[0][:, j * SIDE:(j + 1) * SIDE]
                    im = parts[1][:, j * SIDE:(j + 1) * SIDE]
                    lane = a * bands + j
                    cb = cu[:, lane:lane + 1]
                    sb = su[:, lane:lane + 1]
                    cv = slant_tab[0, pl.ds(b, 1), :]
                    sv = slant_tab[1, pl.ds(b, 1), :]
                    cosine = cb * cv - sb * sv
                    sine = sb * cv + cb * sv
                    demod = jnp.concatenate([re * cosine - im * sine, re * sine + im * cosine], axis=0)
                    place = (band // 2) * (2 * tilts) + a * 2 + j
                    sums[place + 1] = sums[chain_ref[b]] + demod
            return carry

        lax.fori_loop(0, half // 2, late_step, 0)

    def tile_sum(o):
        return sums[chain_ref[blocks + o]]

    def to_partner(z, carry):
        pair_out[z] = tile_sum(z * 2 + 1 - core).astype(BF16)
        return carry

    lax.fori_loop(0, layers, to_partner, 0)
    pair_copy = pltpu.make_async_remote_copy(
        src_ref=pair_out, dst_ref=pair_in, send_sem=pair_send, recv_sem=pair_recv,
        device_id=(partner, me), device_id_type=MESH,
    )
    pair_copy.start()
    pair_copy.wait_recv()

    def far_copy(d):
        to = (layer + d) % layers
        return pltpu.make_async_remote_copy(
            src_ref=far_out.at[d - 1], dst_ref=far_in.at[d - 1],
            send_sem=far_send.at[d - 1], recv_sem=far_recv.at[d - 1],
            device_id=(to * 2 + core, me), device_id_type=MESH,
        )

    for d in range(1, layers):
        z = (layer + d) % layers
        far_out[d - 1] = (tile_sum(z * 2 + core) + pair_in[z].astype(F32)).astype(BF16)
        far_copy(d).start()
    own[...] = tile_sum(layer * 2 + core) + pair_in[layer].astype(F32)
    for d in range(1, layers):
        far_copy(d).wait_recv()
        own[...] += far_in[d - 1].astype(F32)

    total = own[...].astype(BF16)
    total = jnp.concatenate([total[:SIDE], total[SIDE:]], axis=1)
    rows_done = jnp.dot(stencils[0], total, preferred_element_type=F32).astype(BF16)
    rows_done = jnp.concatenate([rows_done[:, :SIDE], rows_done[:, SIDE:]], axis=0)
    tile = lax.dot_general(rows_done, stencils[1], (((1,), (1,)), ((), ())), preferred_element_type=F32)
    out_ref[...] = (0.25 * tile).astype(BF16)

    def sent(q, carry):
        for piece in range(PIECES):
            for d in range(1, members):
                mem_copy(q, piece, d).wait_send()
        return carry

    lax.fori_loop(0, chunks, sent, 0)
    pair_copy.wait_send()
    for d in range(1, layers):
        far_copy(d).wait_send()


def block_chain(owners, groups, tilts):
    blocks = owners.shape[0]
    bands = blocks // tilts
    keys = jnp.concatenate([owners, jnp.arange(groups, dtype=I32)])

    def place(block):
        tilt, band = block // bands, block % bands
        return (band // 2) * (2 * tilts) + tilt * 2 + band % 2

    row = jnp.arange(blocks + groups, dtype=I32)[:, None]
    row = jnp.where(row < blocks, place(row), blocks)
    column = place(jnp.arange(blocks, dtype=I32)[None, :])
    follows = (keys[:, None] == owners[None, :]) & (column < row)
    return jnp.max(jnp.where(follows, column + 1, 0), axis=1)


def on_device(echo, angles, holder, slopes, lead, weight, *, groups, members):
    _, _, sweeps, frequencies = echo.shape
    _, _, angle_count, all_sweeps = angles.shape
    coarse = frequencies // SIDE
    half = coarse // members // PIECES
    chunks = sweeps // CHUNK
    tilts = angle_count // SIDE
    blocks = slopes.shape[3]
    layers = groups // 2
    exchange = (members, chunks, PIECES, 2, half, CHUNK, SIDE)
    vmem = pl.BlockSpec(memory_space=pltpu.VMEM)
    anywhere = pl.BlockSpec(memory_space=pl.ANY)
    dma = pltpu.SemaphoreType.DMA
    tile = pl.pallas_call(
        functools.partial(kernel, groups, members),
        out_shape=jax.ShapeDtypeStruct((2 * SIDE, SIDE), BF16),
        in_specs=[pl.BlockSpec(memory_space=pltpu.SMEM), anywhere, anywhere, vmem, vmem, vmem],
        out_specs=vmem,
        scratch_shapes=[
            pltpu.VMEM((2, sweeps, frequencies), BF16),
            pltpu.VMEM((angle_count, all_sweeps), F32),
            pltpu.VMEM((2 * coarse * CHUNK, SIDE), F32),
            pltpu.VMEM((2 * coarse * CHUNK, SIDE), F32),
            pltpu.VMEM((2 * coarse, 2 * coarse), BF16),
            pltpu.VMEM((2 * coarse, 2 * SIDE), BF16),
            pltpu.VMEM((2, SIDE, SIDE), F32),
            pltpu.VMEM(exchange, BF16),
            pltpu.VMEM(exchange, BF16),
            pltpu.VMEM((tilts, 2, SIDE, 2 * all_sweeps), BF16),
            pltpu.VMEM((PIECES * (half // 2), tilts, 2, SIDE, 2 * SIDE), F32),
            pltpu.VMEM((blocks + 1, 2 * SIDE, SIDE), F32),
            pltpu.VMEM((2, SIDE, SIDE), F32),
            pltpu.VMEM((2, SIDE, SIDE), F32),
            pltpu.VMEM((2, SIDE, SIDE), BF16),
            pltpu.VMEM((layers, 2 * SIDE, SIDE), BF16),
            pltpu.VMEM((layers, 2 * SIDE, SIDE), BF16),
            pltpu.VMEM((layers - 1, 2 * SIDE, SIDE), BF16),
            pltpu.VMEM((layers - 1, 2 * SIDE, SIDE), BF16),
            pltpu.VMEM((2 * SIDE, SIDE), F32),
            dma((chunks,)),
            dma,
            dma((members - 1, chunks, PIECES)),
            dma((members - 1, chunks, PIECES)),
            dma,
            dma,
            dma((layers - 1,)),
            dma((layers - 1,)),
        ],
        compiler_params=pltpu.CompilerParams(
            vmem_limit_bytes=VMEM_LIMIT, collective_id=0, has_side_effects=True
        ),
    )(block_chain(holder[0, 0], groups, tilts), echo[0], angles[0, 0], slopes[0, 0], lead[0, 0], weight[0, 0])
    return tile.reshape(1, 2, SIDE, SIDE)


def solution(mesh):
    return jax.shard_map(
        functools.partial(on_device, groups=mesh.shape["sub"], members=mesh.shape["mem"]),
        mesh=mesh,
        in_specs=(
            P("sub", None, "mem", None),
            P("sub", "mem", None, None),
            P("sub", "mem", None),
            P("sub", "mem", None, None),
            P("sub", "mem", None, None),
            P("sub", "mem", None, None),
        ),
        out_specs=P(("sub", "mem"), None, None, None),
        check_vma=False,
    )
```

```python
import functools
import math

import jax
import jax.numpy as jnp
from jax import lax
from jax.experimental import pallas as pl
from jax.experimental.pallas import tpu as pltpu
from jax.sharding import PartitionSpec as P

SIDE = 128
CHUNK = 16
F32 = jnp.float32
BF16 = jnp.bfloat16
I32 = jnp.int32
MESH = pl.DeviceIdType.MESH
VMEM_LIMIT = 56 * 1024 * 1024


def cos_sin(x):
    q = jnp.floor(x * (2.0 / math.pi) + 0.5)
    r = x - q * 1.5703125
    r = r - q * 4.837512969970703e-4
    r = r - q * 7.549789948768648e-8
    z = r * r
    s = r + r * z * (-1.6666654611e-1 + z * (8.3321608736e-3 + z * -1.9515295891e-4))
    c = 1.0 - 0.5 * z + z * z * (4.166664568298827e-2 + z * (-1.388731625493765e-3 + z * 2.443315711809948e-5))
    n = q.astype(jnp.int32)
    odd = (n & 1) == 1
    cos_base = jnp.where(odd, s, c)
    sin_base = jnp.where(odd, c, s)
    cos_neg = ((n + 1) & 2) == 2
    sin_neg = (n & 2) == 2
    return jnp.where(cos_neg, -cos_base, cos_base), jnp.where(sin_neg, -sin_base, sin_base)


def iota(rows, columns, dimension):
    return lax.broadcasted_iota(I32, (rows, columns), dimension)


def stacked_transform(coarse, columns):
    turns = (iota(coarse, columns, 0) * iota(coarse, columns, 1)) & (coarse - 1)
    c, s = cos_sin(turns.astype(F32) * (2.0 * math.pi / coarse))
    top = jnp.concatenate([c, -s], axis=1)
    low = jnp.concatenate([s, c], axis=1)
    return jnp.concatenate([top, low], axis=0).astype(BF16)


def down(row):
    return jnp.transpose(jnp.broadcast_to(row, (SIDE, SIDE)))


def stencil(lead_row, weight_row):
    f = down(weight_row)
    taps = [
        -f * (f - 1.0) * (f - 2.0) / 6.0,
        (f + 1.0) * (f - 1.0) * (f - 2.0) / 2.0,
        -(f + 1.0) * f * (f - 2.0) / 2.0,
        (f + 1.0) * f * (f - 1.0) / 6.0,
    ]
    distance = iota(SIDE, SIDE, 1).astype(F32) - down(lead_row.astype(F32))
    total = jnp.zeros((SIDE, SIDE), F32)
    for q in range(4):
        total = total + jnp.where(distance == q, taps[q], 0.0)
    return total.astype(BF16)


def kernel(
    groups, members,
    owner_ref, x_hbm, angle_hbm, slope_ref, lead_ref, weight_ref, out_ref,
    x, angle, xs, ys, w1s, w2s, turn, send, recv, lhs, polar, sums, phase, row_tab, chain_rows, chain_ref, slant_tab, stencils,
    pair_out, pair_in, far_out, far_in, own,
    x_sem, angle_sem, chain_sem, mem_send, mem_recv, pair_send, pair_recv, far_send, far_recv,
):
    layers = groups // 2
    _, sweeps, frequencies = x.shape
    coarse = frequencies // SIDE
    bands = coarse // members
    pieces = send.shape[2]
    half = bands // pieces
    chunks = sweeps // CHUNK
    angles, all_sweeps = angle.shape
    tilts = angles // SIDE
    depth = 2 * members * CHUNK
    sub = lax.axis_index("sub")
    me = lax.axis_index("mem")
    layer, core = sub // 2, sub % 2
    partner = layer * 2 + 1 - core

    barrier = pltpu.get_barrier_semaphore()
    for d in range(1, members):
        pl.semaphore_signal(barrier, inc=1, device_id=(sub, (me + d) % members), device_id_type=MESH)
    pl.semaphore_signal(barrier, inc=1, device_id=(partner, me), device_id_type=MESH)
    for d in range(1, layers):
        other = ((layer + d) % layers) * 2 + core
        pl.semaphore_signal(barrier, inc=1, device_id=(other, me), device_id_type=MESH)

    def x_copy(q):
        rows = pl.ds(pl.multiple_of(q * CHUNK, CHUNK), CHUNK)
        return pltpu.make_async_copy(x_hbm.at[:, rows, :], x.at[:, rows, :], x_sem.at[q])

    for q in range(chunks):
        x_copy(q).start()
    angle_copy = pltpu.make_async_copy(angle_hbm, angle, angle_sem)
    angle_copy.start()

    w1s[...] = stacked_transform(coarse, coarse)
    w2s[...] = stacked_transform(coarse, SIDE)
    c, s = cos_sin((iota(SIDE, SIDE, 0) * iota(SIDE, SIDE, 1)).astype(F32) * (2.0 * math.pi / frequencies))
    turn[0] = c * (1.0 / math.sqrt(frequencies))
    turn[1] = s * (1.0 / math.sqrt(frequencies))

    def mem_copies(q, d, only=None):
        to = (me + d) % members
        parts = [None] if q < chunks - 1 else range(pieces) if only is None else [only]
        return [
            pltpu.make_async_remote_copy(
                src_ref=send.at[to, q] if piece is None else send.at[to, q, piece],
                dst_ref=recv.at[me, q] if piece is None else recv.at[me, q, piece],
                send_sem=mem_send.at[d - 1, q, piece or 0],
                recv_sem=mem_recv.at[d - 1, q, piece or 0],
                device_id=(sub, to),
                device_id_type=MESH,
            )
            for piece in parts
        ]

    def transform(q):
        x_copy(q).wait()
        rows = slice(q * CHUNK, (q + 1) * CHUNK)

        def spread(k2, inner):
            lanes = pl.ds(pl.multiple_of(k2 * SIDE, SIDE), SIDE)
            for p in range(2):
                at = pl.ds(pl.multiple_of((p * coarse + k2) * CHUNK, CHUNK), CHUNK)
                xs[at, :] = x[p, rows, lanes].astype(F32)
            return inner

        lax.fori_loop(0, coarse, spread, 0, unroll=8)

        batch = 8

        def sweep_batch(step, inner):
            w1 = w1s[...]
            w2 = w2s[...]
            for j in range(0, batch, 2):
                at = [pl.ds(step * batch + j + h, 2 * coarse, stride=CHUNK) for h in range(2)]
                both = jnp.concatenate([xs[at[h], :].astype(BF16) for h in range(2)], axis=1)
                f = jnp.dot(w1, both, preferred_element_type=F32)
                turned = []
                for h in range(2):
                    part = f[:, h * SIDE:(h + 1) * SIDE]
                    re = jnp.concatenate([part[:coarse], part[:coarse]], axis=0)
                    im = jnp.concatenate([part[coarse:], part[coarse:]], axis=0)
                    cosine, sine = turn[0], turn[1]
                    turned.append(jnp.concatenate(
                        [(re * cosine - im * sine).astype(BF16), (re * sine + im * cosine).astype(BF16)], axis=1
                    ))
                y = lax.dot_general(
                    w2, jnp.concatenate(turned, axis=0), (((1,), (1,)), ((), ())), preferred_element_type=F32
                )
                for h in range(2):
                    ys[at[h], :] = y[:, h * SIDE:(h + 1) * SIDE]
            return inner

        lax.fori_loop(0, CHUNK // batch, sweep_batch, 0)

        def pack(m, inner):
            for piece in range(pieces):
                for p in range(2):
                    for band in range(half):
                        row = (p * coarse + m * bands + piece * half + band) * CHUNK
                        send[m, q, piece, p, band] = ys[pl.ds(pl.multiple_of(row, CHUNK), CHUNK), :].astype(BF16)
            return inner

        lax.fori_loop(0, members, pack, 0)

    for q in range(chunks):
        transform(q)
        if q == 0:
            pl.semaphore_wait(barrier, (members - 1) + 1 + (layers - 1))
        copies = [mem_copies(q, d) for d in range(1, members)]
        for group in zip(*copies):
            for copy in group:
                copy.start()

    angle_copy.wait()
    factor = 1.0 / math.sqrt(all_sweeps)
    wide = 2 * all_sweeps
    source = iota(wide, wide, 0)
    k = iota(wide, wide, 1)
    q_of, p_of = k // depth, (k // (depth // 2)) % 2
    position = ((k // CHUNK) % members) * sweeps + q_of * CHUNK + k % CHUNK
    cos_at = (source == position).astype(F32)
    sin_at = (source == position + all_sweeps).astype(F32)
    first = p_of == 0
    place_re = jnp.where(first, cos_at, -sin_at).astype(BF16)
    place_im = jnp.where(first, sin_at, cos_at).astype(BF16)
    for a in range(tilts):
        c, s = cos_sin(angle[a * SIDE:(a + 1) * SIDE, :])
        table = jnp.concatenate([(c * factor).astype(BF16), (s * factor).astype(BF16)], axis=1)
        lhs[a, 0] = jnp.dot(table, place_re, preferred_element_type=F32).astype(BF16)
        lhs[a, 1] = jnp.dot(table, place_im, preferred_element_type=F32).astype(BF16)

    blocks = slope_ref.shape[1]
    row_tab[...] = jnp.zeros_like(row_tab)
    row_tab[0:2, :blocks] = slope_ref[...]
    row_tab[2:3, :blocks] = owner_ref[...].astype(F32)

    def place(block):
        tilt, band = block // bands, block % bands
        return (band // 2) * (2 * tilts) + tilt * 2 + band % 2

    owner_row = row_tab[2:3, :]
    lane = iota(SIDE, SIDE, 1)
    taken = iota(SIDE, SIDE, 0)
    key = jnp.where(lane < blocks, jnp.broadcast_to(owner_row, (SIDE, SIDE)), (lane - blocks).astype(F32))
    limit = jnp.where(lane < blocks, place(lane), blocks)
    earlier = place(taken)
    follows = (key == down(owner_row)) & (taken < blocks) & (earlier < limit)
    chain = jnp.max(jnp.where(follows, earlier + 1, 0), axis=0, keepdims=True)
    chain_rows[...] = jnp.broadcast_to(chain, chain_rows.shape)
    chain_copy = pltpu.make_async_copy(chain_rows, chain_ref, chain_sem)
    chain_copy.start()

    c, s = cos_sin(iota(SIDE, SIDE, 1).astype(F32) * down(row_tab[1:2, :]))
    slant_tab[0] = c
    slant_tab[1] = s
    tilt_cos, tilt_sin = cos_sin(iota(SIDE, SIDE, 0).astype(F32) * row_tab[0:1, :])
    for b in range(blocks):
        cb = tilt_cos[:, b:b + 1]
        sb = tilt_sin[:, b:b + 1]
        cv = slant_tab[0, b:b + 1, :]
        sv = slant_tab[1, b:b + 1, :]
        phase[b, 0] = cb * cv - sb * sv
        phase[b, 1] = sb * cv + cb * sv
    for d in range(2):
        stencils[d] = stencil(lead_ref[d:d + 1, :], weight_ref[d:d + 1, :])
    sums[0] = jnp.zeros((2 * SIDE, SIDE), F32)

    def keep_own(q, carry):
        recv[me, q] = send[me, q]
        return carry

    lax.fori_loop(0, chunks, keep_own, 0)

    def columns(piece, i, q):
        return jnp.concatenate(
            [
                jnp.concatenate([recv[m, q, piece, p, i * 2 + j] for j in range(2)], axis=1)
                for p in range(2)
                for m in range(members)
            ],
            axis=0,
        )

    held = max(chunks - 2, 0)
    early = held * depth
    if held:
        for q in range(held):
            for d in range(1, members):
                for copy in mem_copies(q, d):
                    copy.wait_recv()
        for piece in range(pieces):
            def early_step(i, carry, piece=piece):
                rhs = jnp.concatenate([columns(piece, i, q) for q in range(held)], axis=0)
                for a in range(tilts):
                    for r in range(2):
                        polar[piece * (half // 2) + i, a, r] = jnp.dot(
                            lhs[a, r, :, :early], rhs, preferred_element_type=F32
                        )
                return carry

            lax.fori_loop(0, half // 2, early_step, 0)

    chain_copy.wait()
    for q in range(held, chunks - 1):
        for d in range(1, members):
            for copy in mem_copies(q, d):
                copy.wait_recv()
    for piece in range(pieces):
        for d in range(1, members):
            mem_copies(chunks - 1, d, piece)[0].wait_recv()

        def late_step(i, carry, piece=piece):
            rhs = jnp.concatenate([columns(piece, i, q) for q in range(held, chunks)], axis=0)
            band = piece * half + i * 2
            for a in range(tilts):
                parts = []
                for r in range(2):
                    part = jnp.dot(lhs[a, r, :, early:], rhs, preferred_element_type=F32)
                    if held:
                        part = part + polar[piece * (half // 2) + i, a, r]
                    parts.append(part)
                for j in range(2):
                    b = a * bands + band + j
                    re = parts[0][:, j * SIDE:(j + 1) * SIDE]
                    im = parts[1][:, j * SIDE:(j + 1) * SIDE]
                    cosine = phase[b, 0]
                    sine = phase[b, 1]
                    demod = jnp.concatenate([re * cosine - im * sine, re * sine + im * cosine], axis=0)
                    at = (band // 2) * (2 * tilts) + a * 2 + j
                    sums[at + 1] = sums[chain_ref[0, b]] + demod
            return carry

        lax.fori_loop(0, half // 2, late_step, 0)

    def tile_sum(o):
        return sums[chain_ref[0, blocks + o]]

    def to_partner(z, carry):
        pair_out[z] = tile_sum(z * 2 + 1 - core).astype(BF16)
        return carry

    lax.fori_loop(0, layers, to_partner, 0)
    pair_copy = pltpu.make_async_remote_copy(
        src_ref=pair_out, dst_ref=pair_in, send_sem=pair_send, recv_sem=pair_recv,
        device_id=(partner, me), device_id_type=MESH,
    )
    pair_copy.start()
    pair_copy.wait_recv()

    def far_copy(d):
        to = (layer + d) % layers
        return pltpu.make_async_remote_copy(
            src_ref=far_out.at[d - 1], dst_ref=far_in.at[d - 1],
            send_sem=far_send.at[d - 1], recv_sem=far_recv.at[d - 1],
            device_id=(to * 2 + core, me), device_id_type=MESH,
        )

    for d in range(1, layers):
        z = (layer + d) % layers
        far_out[d - 1] = (tile_sum(z * 2 + core) + pair_in[z].astype(F32)).astype(BF16)
        far_copy(d).start()
    own[...] = tile_sum(layer * 2 + core) + pair_in[layer].astype(F32)
    for d in range(1, layers):
        far_copy(d).wait_recv()
        own[...] += far_in[d - 1].astype(F32)

    total = own[...].astype(BF16)
    total = jnp.concatenate([total[:SIDE], total[SIDE:]], axis=1)
    rows_done = jnp.dot(stencils[0], total, preferred_element_type=F32).astype(BF16)
    rows_done = jnp.concatenate([rows_done[:, :SIDE], rows_done[:, SIDE:]], axis=0)
    tile = lax.dot_general(rows_done, stencils[1], (((1,), (1,)), ((), ())), preferred_element_type=F32)
    out_ref[...] = tile

    for q in range(chunks):
        for d in range(1, members):
            for copy in mem_copies(q, d):
                copy.wait_send()
    pair_copy.wait_send()
    for d in range(1, layers):
        far_copy(d).wait_send()


def on_device(echo, angles, holder, slopes, lead, weight, *, groups, members):
    _, _, sweeps, frequencies = echo.shape
    _, _, angle_count, all_sweeps = angles.shape
    coarse = frequencies // SIDE
    bands = coarse // members
    pieces = min(4, bands // 2)
    half = bands // pieces
    chunks = sweeps // CHUNK
    tilts = angle_count // SIDE
    blocks = slopes.shape[3]
    layers = groups // 2
    exchange = (members, chunks, pieces, 2, half, CHUNK, SIDE)
    vmem = pl.BlockSpec(memory_space=pltpu.VMEM)
    anywhere = pl.BlockSpec(memory_space=pl.ANY)
    dma = pltpu.SemaphoreType.DMA
    tile = pl.pallas_call(
        functools.partial(kernel, groups, members),
        out_shape=jax.ShapeDtypeStruct((2 * SIDE, SIDE), F32),
        in_specs=[vmem, anywhere, anywhere, vmem, vmem, vmem],
        out_specs=vmem,
        scratch_shapes=[
            pltpu.VMEM((2, sweeps, frequencies), BF16),
            pltpu.VMEM((angle_count, all_sweeps), F32),
            pltpu.VMEM((2 * coarse * CHUNK, SIDE), F32),
            pltpu.VMEM((2 * coarse * CHUNK, SIDE), F32),
            pltpu.VMEM((2 * coarse, 2 * coarse), BF16),
            pltpu.VMEM((2 * coarse, 2 * SIDE), BF16),
            pltpu.VMEM((2, SIDE, SIDE), F32),
            pltpu.VMEM(exchange, BF16),
            pltpu.VMEM(exchange, BF16),
            pltpu.VMEM((tilts, 2, SIDE, 2 * all_sweeps), BF16),
            pltpu.VMEM((bands // 2, tilts, 2, SIDE, 2 * SIDE), F32),
            pltpu.VMEM((blocks + 1, 2 * SIDE, SIDE), F32),
            pltpu.VMEM((blocks, 2, SIDE, SIDE), F32),
            pltpu.VMEM((8, SIDE), F32),
            pltpu.VMEM((8, SIDE), I32),
            pltpu.SMEM((8, SIDE), I32),
            pltpu.VMEM((2, SIDE, SIDE), F32),
            pltpu.VMEM((2, SIDE, SIDE), BF16),
            pltpu.VMEM((layers, 2 * SIDE, SIDE), BF16),
            pltpu.VMEM((layers, 2 * SIDE, SIDE), BF16),
            pltpu.VMEM((layers - 1, 2 * SIDE, SIDE), BF16),
            pltpu.VMEM((layers - 1, 2 * SIDE, SIDE), BF16),
            pltpu.VMEM((2 * SIDE, SIDE), F32),
            dma((chunks,)),
            dma,
            dma,
            dma((members - 1, chunks, pieces)),
            dma((members - 1, chunks, pieces)),
            dma,
            dma,
            dma((layers - 1,)),
            dma((layers - 1,)),
        ],
        compiler_params=pltpu.CompilerParams(
            vmem_limit_bytes=VMEM_LIMIT, collective_id=0, has_side_effects=True
        ),
    )(holder[0], echo[0], angles[0, 0], slopes[0, 0], lead[0, 0], weight[0, 0])
    return (0.25 * tile).astype(BF16).reshape(1, 2, SIDE, SIDE)


def solution(mesh):
    return jax.shard_map(
        functools.partial(on_device, groups=mesh.shape["sub"], members=mesh.shape["mem"]),
        mesh=mesh,
        in_specs=(
            P("sub", None, "mem", None),
            P("sub", "mem", None, None),
            P("sub", "mem", None),
            P("sub", "mem", None, None),
            P("sub", "mem", None, None),
            P("sub", "mem", None, None),
        ),
        out_specs=P(("sub", "mem"), None, None, None),
        check_vma=False,
    )
```

```python
import functools
import math

import jax
import jax.numpy as jnp
from jax import lax
from jax.experimental import pallas as pl
from jax.experimental.pallas import tpu as pltpu
from jax.sharding import PartitionSpec as P

SIDE = 128
CHUNK = 16
F32 = jnp.float32
BF16 = jnp.bfloat16
I32 = jnp.int32
MESH = pl.DeviceIdType.MESH
VMEM_LIMIT = 56 * 1024 * 1024


def cos_sin(x):
    q = jnp.floor(x * (2.0 / math.pi) + 0.5)
    r = x - q * 1.5703125
    r = r - q * 4.837512969970703e-4
    r = r - q * 7.549789948768648e-8
    z = r * r
    s = r + r * z * (-1.6666654611e-1 + z * (8.3321608736e-3 + z * -1.9515295891e-4))
    c = 1.0 - 0.5 * z + z * z * (4.166664568298827e-2 + z * (-1.388731625493765e-3 + z * 2.443315711809948e-5))
    n = q.astype(jnp.int32)
    odd = (n & 1) == 1
    cos_base = jnp.where(odd, s, c)
    sin_base = jnp.where(odd, c, s)
    cos_neg = ((n + 1) & 2) == 2
    sin_neg = (n & 2) == 2
    return jnp.where(cos_neg, -cos_base, cos_base), jnp.where(sin_neg, -sin_base, sin_base)


def iota(rows, columns, dimension):
    return lax.broadcasted_iota(I32, (rows, columns), dimension)


def stacked_transform(coarse, columns):
    turns = (iota(coarse, columns, 0) * iota(coarse, columns, 1)) & (coarse - 1)
    c, s = cos_sin(turns.astype(F32) * (2.0 * math.pi / coarse))
    top = jnp.concatenate([c, -s], axis=1)
    low = jnp.concatenate([s, c], axis=1)
    return jnp.concatenate([top, low], axis=0).astype(BF16)


def down(row):
    return jnp.transpose(jnp.broadcast_to(row, (SIDE, SIDE)))


def stencil(lead_row, weight_row):
    f = down(weight_row)
    taps = [
        -f * (f - 1.0) * (f - 2.0) / 6.0,
        (f + 1.0) * (f - 1.0) * (f - 2.0) / 2.0,
        -(f + 1.0) * f * (f - 2.0) / 2.0,
        (f + 1.0) * f * (f - 1.0) / 6.0,
    ]
    distance = iota(SIDE, SIDE, 1).astype(F32) - down(lead_row.astype(F32))
    total = jnp.zeros((SIDE, SIDE), F32)
    for q in range(4):
        total = total + jnp.where(distance == q, taps[q], 0.0)
    return total.astype(BF16)


def kernel(
    groups, members,
    owner_ref, x_hbm, angle_hbm, slope_ref, lead_ref, weight_ref, out_ref,
    x, angle, xs, ys, w1s, w2s, turn, send, recv, lhs, polar, sums, phase, row_tab, chain_rows, chain_ref, tilt_tab, slant_tab, stencils,
    pair_out, pair_in, far_out, far_in, own,
    x_sem, angle_sem, chain_sem, mem_send, mem_recv, pair_send, pair_recv, far_send, far_recv,
):
    layers = groups // 2
    _, sweeps, frequencies = x.shape
    coarse = frequencies // SIDE
    bands = coarse // members
    pieces = send.shape[2]
    half = bands // pieces
    chunks = sweeps // CHUNK
    angles, all_sweeps = angle.shape
    tilts = angles // SIDE
    depth = 2 * members * CHUNK
    sub = lax.axis_index("sub")
    me = lax.axis_index("mem")
    layer, core = sub // 2, sub % 2
    partner = layer * 2 + 1 - core

    barrier = pltpu.get_barrier_semaphore()
    for d in range(1, members):
        pl.semaphore_signal(barrier, inc=1, device_id=(sub, (me + d) % members), device_id_type=MESH)
    pl.semaphore_signal(barrier, inc=1, device_id=(partner, me), device_id_type=MESH)
    for d in range(1, layers):
        other = ((layer + d) % layers) * 2 + core
        pl.semaphore_signal(barrier, inc=1, device_id=(other, me), device_id_type=MESH)

    def x_copy(q):
        rows = pl.ds(pl.multiple_of(q * CHUNK, CHUNK), CHUNK)
        return pltpu.make_async_copy(x_hbm.at[:, rows, :], x.at[:, rows, :], x_sem.at[q])

    for q in range(chunks):
        x_copy(q).start()
    angle_copy = pltpu.make_async_copy(angle_hbm, angle, angle_sem)
    angle_copy.start()

    w1s[...] = stacked_transform(coarse, coarse)
    w2s[...] = stacked_transform(coarse, SIDE)
    c, s = cos_sin((iota(SIDE, SIDE, 0) * iota(SIDE, SIDE, 1)).astype(F32) * (2.0 * math.pi / frequencies))
    turn[0] = c * (1.0 / math.sqrt(frequencies))
    turn[1] = s * (1.0 / math.sqrt(frequencies))

    def mem_copy(q, piece, d):
        to = (me + d) % members
        return pltpu.make_async_remote_copy(
            src_ref=send.at[to, q, piece],
            dst_ref=recv.at[me, q, piece],
            send_sem=mem_send.at[d - 1, q, piece],
            recv_sem=mem_recv.at[d - 1, q, piece],
            device_id=(sub, to),
            device_id_type=MESH,
        )

    pl.semaphore_wait(barrier, (members - 1) + 1 + (layers - 1))

    def transform(q, carry):
        x_copy(q).wait()
        rows = pl.ds(pl.multiple_of(q * CHUNK, CHUNK), CHUNK)

        def spread(k2, inner):
            lanes = pl.ds(pl.multiple_of(k2 * SIDE, SIDE), SIDE)
            for p in range(2):
                at = pl.ds(pl.multiple_of((p * coarse + k2) * CHUNK, CHUNK), CHUNK)
                xs[at, :] = x[p, rows, lanes].astype(F32)
            return inner

        lax.fori_loop(0, coarse, spread, 0, unroll=8)

        batch = 8

        def sweep_batch(step, inner):
            w1 = w1s[...]
            w2 = w2s[...]
            for j in range(0, batch, 2):
                at = [pl.ds(step * batch + j + h, 2 * coarse, stride=CHUNK) for h in range(2)]
                both = jnp.concatenate([xs[at[h], :].astype(BF16) for h in range(2)], axis=1)
                f = jnp.dot(w1, both, preferred_element_type=F32)
                turned = []
                for h in range(2):
                    part = f[:, h * SIDE:(h + 1) * SIDE]
                    re = jnp.concatenate([part[:coarse], part[:coarse]], axis=0)
                    im = jnp.concatenate([part[coarse:], part[coarse:]], axis=0)
                    cosine, sine = turn[0], turn[1]
                    turned.append(jnp.concatenate(
                        [(re * cosine - im * sine).astype(BF16), (re * sine + im * cosine).astype(BF16)], axis=1
                    ))
                y = lax.dot_general(
                    w2, jnp.concatenate(turned, axis=0), (((1,), (1,)), ((), ())), preferred_element_type=F32
                )
                for h in range(2):
                    ys[at[h], :] = y[:, h * SIDE:(h + 1) * SIDE]
            return inner

        lax.fori_loop(0, CHUNK // batch, sweep_batch, 0)

        def pack(m, inner):
            for piece in range(pieces):
                for p in range(2):
                    for band in range(half):
                        row = (p * coarse + m * bands + piece * half + band) * CHUNK
                        send[m, q, piece, p, band] = ys[pl.ds(pl.multiple_of(row, CHUNK), CHUNK), :].astype(BF16)
            return inner

        lax.fori_loop(0, members, pack, 0)

        for piece in range(pieces):
            for d in range(1, members):
                mem_copy(q, piece, d).start()
        return carry

    lax.fori_loop(0, chunks, transform, 0)

    angle_copy.wait()
    factor = 1.0 / math.sqrt(all_sweeps)
    wide = 2 * all_sweeps
    source = iota(wide, wide, 0)
    k = iota(wide, wide, 1)
    q_of, p_of = k // depth, (k // (depth // 2)) % 2
    position = ((k // CHUNK) % members) * sweeps + q_of * CHUNK + k % CHUNK
    cos_at = (source == position).astype(F32)
    sin_at = (source == position + all_sweeps).astype(F32)
    first = p_of == 0
    place_re = jnp.where(first, cos_at, -sin_at).astype(BF16)
    place_im = jnp.where(first, sin_at, cos_at).astype(BF16)
    for a in range(tilts):
        c, s = cos_sin(angle[a * SIDE:(a + 1) * SIDE, :])
        table = jnp.concatenate([(c * factor).astype(BF16), (s * factor).astype(BF16)], axis=1)
        lhs[a, 0] = jnp.dot(table, place_re, preferred_element_type=F32).astype(BF16)
        lhs[a, 1] = jnp.dot(table, place_im, preferred_element_type=F32).astype(BF16)

    blocks = slope_ref.shape[1]
    row_tab[...] = jnp.zeros_like(row_tab)
    row_tab[0:2, :blocks] = slope_ref[...]
    row_tab[2:3, :blocks] = owner_ref[...].astype(F32)

    def place(block):
        tilt, band = block // bands, block % bands
        return (band // 2) * (2 * tilts) + tilt * 2 + band % 2

    owner_row = row_tab[2:3, :]
    lane = iota(SIDE, SIDE, 1)
    taken = iota(SIDE, SIDE, 0)
    key = jnp.where(lane < blocks, jnp.broadcast_to(owner_row, (SIDE, SIDE)), (lane - blocks).astype(F32))
    limit = jnp.where(lane < blocks, place(lane), blocks)
    earlier = place(taken)
    follows = (key == down(owner_row)) & (taken < blocks) & (earlier < limit)
    chain = jnp.max(jnp.where(follows, earlier + 1, 0), axis=0, keepdims=True)
    chain_rows[...] = jnp.broadcast_to(chain, chain_rows.shape)
    chain_copy = pltpu.make_async_copy(chain_rows, chain_ref, chain_sem)
    chain_copy.start()

    c, s = cos_sin(iota(SIDE, SIDE, 1).astype(F32) * down(row_tab[1:2, :]))
    slant_tab[0] = c
    slant_tab[1] = s
    tilt_cos, tilt_sin = cos_sin(iota(SIDE, SIDE, 0).astype(F32) * row_tab[0:1, :])
    tilt_tab[0] = tilt_cos
    tilt_tab[1] = tilt_sin

    def make_phase(band, carry):
        shift = (SIDE - band) % SIDE
        cu = pltpu.roll(tilt_tab[0], shift, 1)
        su = pltpu.roll(tilt_tab[1], shift, 1)
        for a in range(tilts):
            b = a * bands + band
            cb = cu[:, a * bands:a * bands + 1]
            sb = su[:, a * bands:a * bands + 1]
            cv = slant_tab[0, pl.ds(b, 1), :]
            sv = slant_tab[1, pl.ds(b, 1), :]
            phase[b, 0] = cb * cv - sb * sv
            phase[b, 1] = sb * cv + cb * sv
        return carry

    lax.fori_loop(0, bands, make_phase, 0)
    for d in range(2):
        stencils[d] = stencil(lead_ref[d:d + 1, :], weight_ref[d:d + 1, :])
    sums[0] = jnp.zeros((2 * SIDE, SIDE), F32)

    def keep_own(q, carry):
        recv[me, q] = send[me, q]
        return carry

    lax.fori_loop(0, chunks, keep_own, 0)

    def columns(piece, i, q):
        return jnp.concatenate(
            [
                jnp.concatenate([recv[m, q, piece, p, i * 2 + j] for j in range(2)], axis=1)
                for p in range(2)
                for m in range(members)
            ],
            axis=0,
        )

    held = max(chunks - 2, 0)
    early = held * depth

    def arrived(q, carry):
        for piece in range(pieces):
            for d in range(1, members):
                mem_copy(q, piece, d).wait_recv()
        return carry

    pairs = half // 2
    if held:
        lax.fori_loop(0, held, arrived, 0)

        def early_step(n, carry):
            rhs = jnp.concatenate([columns(n // pairs, n % pairs, q) for q in range(held)], axis=0)
            for a in range(tilts):
                for r in range(2):
                    polar[n, a, r] = jnp.dot(lhs[a, r, :, :early], rhs, preferred_element_type=F32)
            return carry

        lax.fori_loop(0, bands // 2, early_step, 0)

    chain_copy.wait()
    lax.fori_loop(held, chunks - 1, arrived, 0)

    def late_piece(piece, carry):
        for d in range(1, members):
            mem_copy(chunks - 1, piece, d).wait_recv()

        def late_step(i, inner):
            n = piece * pairs + i
            rhs = jnp.concatenate([columns(piece, i, q) for q in range(held, chunks)], axis=0)
            for a in range(tilts):
                parts = []
                for r in range(2):
                    part = jnp.dot(lhs[a, r, :, early:], rhs, preferred_element_type=F32)
                    if held:
                        part = part + polar[n, a, r]
                    parts.append(part)
                for j in range(2):
                    b = a * bands + n * 2 + j
                    re = parts[0][:, j * SIDE:(j + 1) * SIDE]
                    im = parts[1][:, j * SIDE:(j + 1) * SIDE]
                    cosine = phase[b, 0]
                    sine = phase[b, 1]
                    demod = jnp.concatenate([re * cosine - im * sine, re * sine + im * cosine], axis=0)
                    sums[n * (2 * tilts) + a * 2 + j + 1] = sums[chain_ref[0, b]] + demod
            return inner

        lax.fori_loop(0, pairs, late_step, 0)
        return carry

    lax.fori_loop(0, pieces, late_piece, 0)

    def tile_sum(o):
        return sums[chain_ref[0, blocks + o]]

    def pair_copy(d):
        return pltpu.make_async_remote_copy(
            src_ref=pair_out.at[d], dst_ref=pair_in.at[d], send_sem=pair_send.at[d], recv_sem=pair_recv.at[d],
            device_id=(partner, me), device_id_type=MESH,
        )

    order = list(range(1, layers)) + [0]
    for d in order:
        pair_out[d] = tile_sum(((layer + d) % layers) * 2 + 1 - core).astype(BF16)
        pair_copy(d).start()

    def far_copy(d):
        to = (layer + d) % layers
        return pltpu.make_async_remote_copy(
            src_ref=far_out.at[d - 1], dst_ref=far_in.at[d - 1],
            send_sem=far_send.at[d - 1], recv_sem=far_recv.at[d - 1],
            device_id=(to * 2 + core, me), device_id_type=MESH,
        )

    for d in range(1, layers):
        mine = tile_sum(((layer + d) % layers) * 2 + core)
        pair_copy(d).wait_recv()
        far_out[d - 1] = (mine + pair_in[d].astype(F32)).astype(BF16)
        far_copy(d).start()
    pair_copy(0).wait_recv()
    own[...] = tile_sum(layer * 2 + core) + pair_in[0].astype(F32)
    for d in range(1, layers):
        far_copy(d).wait_recv()
        own[...] += far_in[d - 1].astype(F32)

    total = own[...].astype(BF16)
    total = jnp.concatenate([total[:SIDE], total[SIDE:]], axis=1)
    rows_done = jnp.dot(stencils[0], total, preferred_element_type=F32).astype(BF16)
    rows_done = jnp.concatenate([rows_done[:, :SIDE], rows_done[:, SIDE:]], axis=0)
    tile = lax.dot_general(rows_done, stencils[1], (((1,), (1,)), ((), ())), preferred_element_type=F32)
    out_ref[...] = tile

    def sent(q, carry):
        for piece in range(pieces):
            for d in range(1, members):
                mem_copy(q, piece, d).wait_send()
        return carry

    lax.fori_loop(0, chunks, sent, 0)
    for d in order:
        pair_copy(d).wait_send()
    for d in range(1, layers):
        far_copy(d).wait_send()


def on_device(echo, angles, holder, slopes, lead, weight, *, groups, members):
    _, _, sweeps, frequencies = echo.shape
    _, _, angle_count, all_sweeps = angles.shape
    coarse = frequencies // SIDE
    bands = coarse // members
    pieces = min(4, bands // 2)
    half = bands // pieces
    chunks = sweeps // CHUNK
    tilts = angle_count // SIDE
    blocks = slopes.shape[3]
    layers = groups // 2
    exchange = (members, chunks, pieces, 2, half, CHUNK, SIDE)
    vmem = pl.BlockSpec(memory_space=pltpu.VMEM)
    anywhere = pl.BlockSpec(memory_space=pl.ANY)
    dma = pltpu.SemaphoreType.DMA
    tile = pl.pallas_call(
        functools.partial(kernel, groups, members),
        out_shape=jax.ShapeDtypeStruct((2 * SIDE, SIDE), F32),
        in_specs=[vmem, anywhere, anywhere, vmem, vmem, vmem],
        out_specs=vmem,
        scratch_shapes=[
            pltpu.VMEM((2, sweeps, frequencies), BF16),
            pltpu.VMEM((angle_count, all_sweeps), F32),
            pltpu.VMEM((2 * coarse * CHUNK, SIDE), F32),
            pltpu.VMEM((2 * coarse * CHUNK, SIDE), F32),
            pltpu.VMEM((2 * coarse, 2 * coarse), BF16),
            pltpu.VMEM((2 * coarse, 2 * SIDE), BF16),
            pltpu.VMEM((2, SIDE, SIDE), F32),
            pltpu.VMEM(exchange, BF16),
            pltpu.VMEM(exchange, BF16),
            pltpu.VMEM((tilts, 2, SIDE, 2 * all_sweeps), BF16),
            pltpu.VMEM((bands // 2, tilts, 2, SIDE, 2 * SIDE), F32),
            pltpu.VMEM((blocks + 1, 2 * SIDE, SIDE), F32),
            pltpu.VMEM((blocks, 2, SIDE, SIDE), F32),
            pltpu.VMEM((8, SIDE), F32),
            pltpu.VMEM((8, SIDE), I32),
            pltpu.SMEM((8, SIDE), I32),
            pltpu.VMEM((2, SIDE, SIDE), F32),
            pltpu.VMEM((2, SIDE, SIDE), F32),
            pltpu.VMEM((2, SIDE, SIDE), BF16),
            pltpu.VMEM((layers, 2 * SIDE, SIDE), BF16),
            pltpu.VMEM((layers, 2 * SIDE, SIDE), BF16),
            pltpu.VMEM((layers - 1, 2 * SIDE, SIDE), BF16),
            pltpu.VMEM((layers - 1, 2 * SIDE, SIDE), BF16),
            pltpu.VMEM((2 * SIDE, SIDE), F32),
            dma((chunks,)),
            dma,
            dma,
            dma((members - 1, chunks, pieces)),
            dma((members - 1, chunks, pieces)),
            dma((layers,)),
            dma((layers,)),
            dma((layers - 1,)),
            dma((layers - 1,)),
        ],
        compiler_params=pltpu.CompilerParams(
            vmem_limit_bytes=VMEM_LIMIT, collective_id=0, has_side_effects=True
        ),
    )(holder[0], echo[0], angles[0, 0], slopes[0, 0], lead[0, 0], weight[0, 0])
    return (0.25 * tile).astype(BF16).reshape(1, 2, SIDE, SIDE)


def solution(mesh):
    return jax.shard_map(
        functools.partial(on_device, groups=mesh.shape["sub"], members=mesh.shape["mem"]),
        mesh=mesh,
        in_specs=(
            P("sub", None, "mem", None),
            P("sub", "mem", None, None),
            P("sub", "mem", None),
            P("sub", "mem", None, None),
            P("sub", "mem", None, None),
            P("sub", "mem", None, None),
        ),
        out_specs=P(("sub", "mem"), None, None, None),
        check_vma=False,
    )
```

```python
import functools
import math

import jax
import jax.numpy as jnp
from jax import lax
from jax.experimental import pallas as pl
from jax.experimental.pallas import tpu as pltpu
from jax.sharding import PartitionSpec as P

SIDE = 128
CHUNK = 16
F32 = jnp.float32
BF16 = jnp.bfloat16
I32 = jnp.int32
MESH = pl.DeviceIdType.MESH
VMEM_LIMIT = 56 * 1024 * 1024


def cos_sin(x):
    q = jnp.floor(x * (2.0 / math.pi) + 0.5)
    r = x - q * 1.5703125
    r = r - q * 4.837512969970703e-4
    r = r - q * 7.549789948768648e-8
    z = r * r
    s = r + r * z * (-1.6666654611e-1 + z * (8.3321608736e-3 + z * -1.9515295891e-4))
    c = 1.0 - 0.5 * z + z * z * (4.166664568298827e-2 + z * (-1.388731625493765e-3 + z * 2.443315711809948e-5))
    n = q.astype(jnp.int32)
    odd = (n & 1) == 1
    cos_base = jnp.where(odd, s, c)
    sin_base = jnp.where(odd, c, s)
    cos_neg = ((n + 1) & 2) == 2
    sin_neg = (n & 2) == 2
    return jnp.where(cos_neg, -cos_base, cos_base), jnp.where(sin_neg, -sin_base, sin_base)


def iota(rows, columns, dimension):
    return lax.broadcasted_iota(I32, (rows, columns), dimension)


def stacked_transform(coarse, columns):
    turns = (iota(coarse, columns, 0) * iota(coarse, columns, 1)) & (coarse - 1)
    c, s = cos_sin(turns.astype(F32) * (2.0 * math.pi / coarse))
    top = jnp.concatenate([c, -s], axis=1)
    low = jnp.concatenate([s, c], axis=1)
    return jnp.concatenate([top, low], axis=0).astype(BF16)


def down(row):
    return jnp.transpose(jnp.broadcast_to(row, (SIDE, SIDE)))


def stencil(lead_row, weight_row):
    f = down(weight_row)
    taps = [
        -f * (f - 1.0) * (f - 2.0) / 6.0,
        (f + 1.0) * (f - 1.0) * (f - 2.0) / 2.0,
        -(f + 1.0) * f * (f - 2.0) / 2.0,
        (f + 1.0) * f * (f - 1.0) / 6.0,
    ]
    distance = iota(SIDE, SIDE, 1).astype(F32) - down(lead_row.astype(F32))
    total = jnp.zeros((SIDE, SIDE), F32)
    for q in range(4):
        total = total + jnp.where(distance == q, taps[q], 0.0)
    return total.astype(BF16)


def kernel(
    groups, members,
    owner_ref, x_hbm, angle_hbm, slope_ref, lead_ref, weight_ref, out_ref,
    x, angle, xs, ys, w1s, w2s, turn, send0, recv0, send1, recv1, lhs, sums, row_tab, chain_rows, chain_ref, tilt_tab, slant_tab, stencils,
    pair_out, pair_in, far_out, far_in, own,
    x_sem, angle_sem, chain_sem, send_sem0, recv_sem0, send_sem1, recv_sem1, pair_send, pair_recv, far_send, far_recv,
):
    layers = groups // 2
    _, sweeps, frequencies = x.shape
    coarse = frequencies // SIDE
    bands = coarse // members
    pieces = send1.shape[1]
    half = bands // pieces
    chunks = sweeps // CHUNK
    angles, all_sweeps = angle.shape
    tilts = angles // SIDE
    sub = lax.axis_index("sub")
    me = lax.axis_index("mem")
    layer, core = sub // 2, sub % 2
    partner = layer * 2 + 1 - core

    barrier = pltpu.get_barrier_semaphore()
    for d in range(1, members):
        pl.semaphore_signal(barrier, inc=1, device_id=(sub, (me + d) % members), device_id_type=MESH)
    pl.semaphore_signal(barrier, inc=1, device_id=(partner, me), device_id_type=MESH)
    for d in range(1, layers):
        other = ((layer + d) % layers) * 2 + core
        pl.semaphore_signal(barrier, inc=1, device_id=(other, me), device_id_type=MESH)

    def x_copy(q):
        rows = pl.ds(pl.multiple_of(q * CHUNK, CHUNK), CHUNK)
        return pltpu.make_async_copy(x_hbm.at[:, rows, :], x.at[:, rows, :], x_sem.at[q])

    for q in range(chunks):
        x_copy(q).start()
    angle_copy = pltpu.make_async_copy(angle_hbm, angle, angle_sem)
    angle_copy.start()

    w1s[...] = stacked_transform(coarse, coarse)
    w2s[...] = stacked_transform(coarse, SIDE)
    c, s = cos_sin((iota(SIDE, SIDE, 0) * iota(SIDE, SIDE, 1)).astype(F32) * (2.0 * math.pi / frequencies))
    turn[0] = c * (1.0 / math.sqrt(frequencies))
    turn[1] = s * (1.0 / math.sqrt(frequencies))

    def mem_copy(h, n, d):
        to = (me + d) % members
        src, dst = ((send0, recv0), (send1, recv1))[h]
        send_sem, recv_sem = ((send_sem0, recv_sem0), (send_sem1, recv_sem1))[h]
        return pltpu.make_async_remote_copy(
            src_ref=src.at[to, n],
            dst_ref=dst.at[me, n],
            send_sem=send_sem.at[d - 1, n],
            recv_sem=recv_sem.at[d - 1, n],
            device_id=(sub, to),
            device_id_type=MESH,
        )

    pl.semaphore_wait(barrier, (members - 1) + 1 + (layers - 1))

    def transform(q, carry):
        x_copy(q).wait()
        rows = pl.ds(pl.multiple_of(q * CHUNK, CHUNK), CHUNK)

        def spread(k2, inner):
            lanes = pl.ds(pl.multiple_of(k2 * SIDE, SIDE), SIDE)
            for p in range(2):
                at = pl.ds(pl.multiple_of((p * coarse + k2) * CHUNK, CHUNK), CHUNK)
                xs[at, :] = x[p, rows, lanes].astype(F32)
            return inner

        lax.fori_loop(0, coarse, spread, 0, unroll=8)

        batch = 8

        def sweep_batch(step, inner):
            w1 = w1s[...]
            w2 = w2s[...]
            for j in range(0, batch, 2):
                at = [pl.ds(step * batch + j + h, 2 * coarse, stride=CHUNK) for h in range(2)]
                both = jnp.concatenate([xs[at[h], :].astype(BF16) for h in range(2)], axis=1)
                f = jnp.dot(w1, both, preferred_element_type=F32)
                turned = []
                for h in range(2):
                    part = f[:, h * SIDE:(h + 1) * SIDE]
                    re = jnp.concatenate([part[:coarse], part[:coarse]], axis=0)
                    im = jnp.concatenate([part[coarse:], part[coarse:]], axis=0)
                    cosine, sine = turn[0], turn[1]
                    turned.append(jnp.concatenate(
                        [(re * cosine - im * sine).astype(BF16), (re * sine + im * cosine).astype(BF16)], axis=1
                    ))
                y = lax.dot_general(
                    w2, jnp.concatenate(turned, axis=0), (((1,), (1,)), ((), ())), preferred_element_type=F32
                )
                for h in range(2):
                    ys[at[h], :] = y[:, h * SIDE:(h + 1) * SIDE]
            return inner

        lax.fori_loop(0, CHUNK // batch, sweep_batch, 0)

        def pack(band, inner):
            low = iota(CHUNK, SIDE, 1) < SIDE // 2
            piece, local = band // half, band % half
            for m in range(members):
                row = (m * bands + band) * CHUNK
                re = ys[pl.ds(pl.multiple_of(row, CHUNK), CHUNK), :]
                im = ys[pl.ds(pl.multiple_of(coarse * CHUNK + row, CHUNK), CHUNK), :]
                send0[m, q, band] = jnp.where(low, re, pltpu.roll(im, SIDE // 2, 1)).astype(BF16)
                send1[m, piece, q, local] = jnp.where(low, pltpu.roll(re, SIDE // 2, 1), im).astype(BF16)
            return inner

        lax.fori_loop(0, bands, pack, 0, unroll=2)
        for d in range(1, members):
            mem_copy(0, q, d).start()
        return carry

    lax.fori_loop(0, chunks, transform, 0)
    for piece in range(pieces):
        for d in range(1, members):
            mem_copy(1, piece, d).start()

    angle_copy.wait()
    factor = 1.0 / math.sqrt(all_sweeps)
    for a in range(tilts):
        c, s = cos_sin(angle[a * SIDE:(a + 1) * SIDE, :])
        lhs[a, 0] = (c * factor).astype(BF16)
        lhs[a, 1] = (s * factor).astype(BF16)

    blocks = slope_ref.shape[1]
    row_tab[...] = jnp.zeros_like(row_tab)
    row_tab[0:2, :blocks] = slope_ref[...]
    row_tab[2:3, :blocks] = owner_ref[...].astype(F32)

    def place(block):
        tilt, band = block // bands, block % bands
        return (band // 2) * (2 * tilts) + tilt * 2 + band % 2

    owner_row = row_tab[2:3, :]
    lane = iota(SIDE, SIDE, 1)
    taken = iota(SIDE, SIDE, 0)
    key = jnp.where(lane < blocks, jnp.broadcast_to(owner_row, (SIDE, SIDE)), (lane - blocks).astype(F32))
    limit = jnp.where(lane < blocks, place(lane), blocks)
    earlier = place(taken)
    follows = (key == down(owner_row)) & (taken < blocks) & (earlier < limit)
    chain = jnp.max(jnp.where(follows, earlier + 1, 0), axis=0, keepdims=True)
    chain_rows[...] = jnp.broadcast_to(chain, chain_rows.shape)
    chain_copy = pltpu.make_async_copy(chain_rows, chain_ref, chain_sem)
    chain_copy.start()

    part_lane = iota(SIDE, SIDE, 1)
    sign = jnp.where(part_lane < SIDE // 2, -1.0, 1.0)
    for h in range(2):
        across = (part_lane % (SIDE // 2) + h * (SIDE // 2)).astype(F32)
        c, s = cos_sin(across * down(row_tab[1:2, :]))
        for n, table in enumerate([c, s, sign * c, sign * s]):
            slant_tab[h, n] = table
    c, s = cos_sin(iota(SIDE, SIDE, 0).astype(F32) * row_tab[0:1, :])
    tilt_tab[0] = c
    tilt_tab[1] = s
    for d in range(2):
        stencils[d] = stencil(lead_ref[d:d + 1, :], weight_ref[d:d + 1, :])
    for h in range(2):
        sums[h, 0] = jnp.zeros((SIDE, SIDE), F32)

    recv0[me] = send0[me]
    recv1[me] = send1[me]

    def form(h, piece, i):
        n = piece * (half // 2) + i

        def band_rows(j):
            if h == 0:
                return [recv0[m, q, n * 2 + j] for m in range(members) for q in range(chunks)]
            return [recv1[m, piece, q, i * 2 + j] for m in range(members) for q in range(chunks)]

        rhs = jnp.concatenate([jnp.concatenate(band_rows(j), axis=0) for j in range(2)], axis=1)
        shift = (SIDE - n * 2) % SIDE
        cu = pltpu.roll(tilt_tab[0], shift, 1)
        su = pltpu.roll(tilt_tab[1], shift, 1)
        signs = jnp.where(iota(SIDE, SIDE, 1) < SIDE // 2, -1.0, 1.0)
        for a in range(tilts):
            with_cos = jnp.dot(lhs[a, 0], rhs, preferred_element_type=F32)
            with_sin = jnp.dot(lhs[a, 1], rhs, preferred_element_type=F32)
            for j in range(2):
                b = a * bands + n * 2 + j
                lanes = slice(j * SIDE, (j + 1) * SIDE)
                polar = with_cos[:, lanes] + signs * pltpu.roll(with_sin[:, lanes], SIDE // 2, 1)
                at = a * bands + j
                cb = cu[:, at:at + 1]
                sb = su[:, at:at + 1]
                cv, sv, signed_cv, signed_sv = [slant_tab[h, t, pl.ds(b, 1), :] for t in range(4)]
                cosine = cb * cv - sb * sv
                signed_sine = sb * signed_cv + cb * signed_sv
                demod = polar * cosine + pltpu.roll(polar, SIDE // 2, 1) * signed_sine
                sums[h, n * (2 * tilts) + a * 2 + j + 1] = sums[h, chain_ref[0, b]] + demod

    pairs = half // 2

    def form_piece(h, piece):
        def step(i, carry):
            form(h, piece, i)
            return carry

        lax.fori_loop(0, pairs, step, 0)

    def arrived(q, carry):
        for d in range(1, members):
            mem_copy(0, q, d).wait_recv()
        return carry

    def second_piece(piece, carry):
        for d in range(1, members):
            mem_copy(1, piece, d).wait_recv()
        form_piece(1, piece)
        return carry

    def tile_sum(h, o):
        return sums[h, chain_ref[0, blocks + o]]

    def pair_copy(h, d):
        return pltpu.make_async_remote_copy(
            src_ref=pair_out.at[h, d], dst_ref=pair_in.at[h, d],
            send_sem=pair_send.at[h, d], recv_sem=pair_recv.at[h, d],
            device_id=(partner, me), device_id_type=MESH,
        )

    def far_copy(h, d):
        to = (layer + d) % layers
        return pltpu.make_async_remote_copy(
            src_ref=far_out.at[h, d - 1], dst_ref=far_in.at[h, d - 1],
            send_sem=far_send.at[h, d - 1], recv_sem=far_recv.at[h, d - 1],
            device_id=(to * 2 + core, me), device_id_type=MESH,
        )

    order = list(range(1, layers)) + [0]

    def send_pair(h):
        for d in order:
            pair_out[h, d] = tile_sum(h, ((layer + d) % layers) * 2 + 1 - core).astype(BF16)
            pair_copy(h, d).start()

    def send_far(h):
        for d in range(1, layers):
            mine = tile_sum(h, ((layer + d) % layers) * 2 + core)
            pair_copy(h, d).wait_recv()
            far_out[h, d - 1] = (mine + pair_in[h, d].astype(F32)).astype(BF16)
            far_copy(h, d).start()
        pair_copy(h, 0).wait_recv()
        own[h] = tile_sum(h, layer * 2 + core) + pair_in[h, 0].astype(F32)

    chain_copy.wait()
    lax.fori_loop(0, chunks, arrived, 0)

    def first_step(n, carry):
        form(0, n // pairs, n % pairs)
        return carry

    lax.fori_loop(0, bands // 2, first_step, 0)
    send_pair(0)
    second_piece(0, 0)
    send_far(0)
    lax.fori_loop(1, pieces, second_piece, 0)
    send_pair(1)
    send_far(1)
    rows = []
    for h in range(2):
        for d in range(1, layers):
            far_copy(h, d).wait_recv()
            own[h] += far_in[h, d - 1].astype(F32)
        rows.append(jnp.dot(stencils[0], own[h].astype(BF16), preferred_element_type=F32))
    low = iota(SIDE, SIDE, 1) < SIDE // 2
    rows_done = jnp.concatenate(
        [
            jnp.where(low, rows[0], pltpu.roll(rows[1], SIDE // 2, 1)),
            jnp.where(low, pltpu.roll(rows[0], SIDE // 2, 1), rows[1]),
        ],
        axis=0,
    ).astype(BF16)
    tile = lax.dot_general(rows_done, stencils[1], (((1,), (1,)), ((), ())), preferred_element_type=F32)
    out_ref[...] = tile

    for h, count in ((0, chunks), (1, pieces)):
        def sent(n, carry, h=h):
            for d in range(1, members):
                mem_copy(h, n, d).wait_send()
            return carry

        lax.fori_loop(0, count, sent, 0)
        for d in order:
            pair_copy(h, d).wait_send()
        for d in range(1, layers):
            far_copy(h, d).wait_send()


def on_device(echo, angles, holder, slopes, lead, weight, *, groups, members):
    _, _, sweeps, frequencies = echo.shape
    _, _, angle_count, all_sweeps = angles.shape
    coarse = frequencies // SIDE
    bands = coarse // members
    pieces = min(4, bands // 2)
    half = bands // pieces
    chunks = sweeps // CHUNK
    tilts = angle_count // SIDE
    blocks = slopes.shape[3]
    layers = groups // 2
    exchange0 = (members, chunks, bands, CHUNK, SIDE)
    exchange1 = (members, pieces, chunks, half, CHUNK, SIDE)
    vmem = pl.BlockSpec(memory_space=pltpu.VMEM)
    anywhere = pl.BlockSpec(memory_space=pl.ANY)
    dma = pltpu.SemaphoreType.DMA
    tile = pl.pallas_call(
        functools.partial(kernel, groups, members),
        out_shape=jax.ShapeDtypeStruct((2 * SIDE, SIDE), F32),
        in_specs=[vmem, anywhere, anywhere, vmem, vmem, vmem],
        out_specs=vmem,
        scratch_shapes=[
            pltpu.VMEM((2, sweeps, frequencies), BF16),
            pltpu.VMEM((angle_count, all_sweeps), F32),
            pltpu.VMEM((2 * coarse * CHUNK, SIDE), F32),
            pltpu.VMEM((2 * coarse * CHUNK, SIDE), F32),
            pltpu.VMEM((2 * coarse, 2 * coarse), BF16),
            pltpu.VMEM((2 * coarse, 2 * SIDE), BF16),
            pltpu.VMEM((2, SIDE, SIDE), F32),
            pltpu.VMEM(exchange0, BF16),
            pltpu.VMEM(exchange0, BF16),
            pltpu.VMEM(exchange1, BF16),
            pltpu.VMEM(exchange1, BF16),
            pltpu.VMEM((tilts, 2, SIDE, all_sweeps), BF16),
            pltpu.VMEM((2, blocks + 1, SIDE, SIDE), F32),
            pltpu.VMEM((8, SIDE), F32),
            pltpu.VMEM((8, SIDE), I32),
            pltpu.SMEM((8, SIDE), I32),
            pltpu.VMEM((2, SIDE, SIDE), F32),
            pltpu.VMEM((2, 4, SIDE, SIDE), F32),
            pltpu.VMEM((2, SIDE, SIDE), BF16),
            pltpu.VMEM((2, layers, SIDE, SIDE), BF16),
            pltpu.VMEM((2, layers, SIDE, SIDE), BF16),
            pltpu.VMEM((2, layers - 1, SIDE, SIDE), BF16),
            pltpu.VMEM((2, layers - 1, SIDE, SIDE), BF16),
            pltpu.VMEM((2, SIDE, SIDE), F32),
            dma((chunks,)),
            dma,
            dma,
            dma((members - 1, chunks)),
            dma((members - 1, chunks)),
            dma((members - 1, pieces)),
            dma((members - 1, pieces)),
            dma((2, layers)),
            dma((2, layers)),
            dma((2, layers - 1)),
            dma((2, layers - 1)),
        ],
        compiler_params=pltpu.CompilerParams(
            vmem_limit_bytes=VMEM_LIMIT, collective_id=0, has_side_effects=True
        ),
    )(holder[0], echo[0], angles[0, 0], slopes[0, 0], lead[0, 0], weight[0, 0])
    return (0.25 * tile).astype(BF16).reshape(1, 2, SIDE, SIDE)


def solution(mesh):
    return jax.shard_map(
        functools.partial(on_device, groups=mesh.shape["sub"], members=mesh.shape["mem"]),
        mesh=mesh,
        in_specs=(
            P("sub", None, "mem", None),
            P("sub", "mem", None, None),
            P("sub", "mem", None),
            P("sub", "mem", None, None),
            P("sub", "mem", None, None),
            P("sub", "mem", None, None),
        ),
        out_specs=P(("sub", "mem"), None, None, None),
        check_vma=False,
    )
```

```python
import functools
import math

import jax
import jax.numpy as jnp
from jax import lax
from jax.experimental import pallas as pl
from jax.experimental.pallas import tpu as pltpu
from jax.sharding import PartitionSpec as P

SIDE = 128
CHUNK = 16
F32 = jnp.float32
BF16 = jnp.bfloat16
I32 = jnp.int32
MESH = pl.DeviceIdType.MESH
VMEM_LIMIT = 56 * 1024 * 1024


def cos_sin(x):
    q = jnp.floor(x * (2.0 / math.pi) + 0.5)
    r = x - q * 1.5703125
    r = r - q * 4.837512969970703e-4
    r = r - q * 7.549789948768648e-8
    z = r * r
    s = r + r * z * (-1.6666654611e-1 + z * (8.3321608736e-3 + z * -1.9515295891e-4))
    c = 1.0 - 0.5 * z + z * z * (4.166664568298827e-2 + z * (-1.388731625493765e-3 + z * 2.443315711809948e-5))
    n = q.astype(jnp.int32)
    odd = (n & 1) == 1
    cos_base = jnp.where(odd, s, c)
    sin_base = jnp.where(odd, c, s)
    cos_neg = ((n + 1) & 2) == 2
    sin_neg = (n & 2) == 2
    return jnp.where(cos_neg, -cos_base, cos_base), jnp.where(sin_neg, -sin_base, sin_base)


def iota(rows, columns, dimension):
    return lax.broadcasted_iota(I32, (rows, columns), dimension)


def stacked_transform(coarse, columns):
    turns = (iota(coarse, columns, 0) * iota(coarse, columns, 1)) & (coarse - 1)
    c, s = cos_sin(turns.astype(F32) * (2.0 * math.pi / coarse))
    top = jnp.concatenate([c, -s], axis=1)
    low = jnp.concatenate([s, c], axis=1)
    return jnp.concatenate([top, low], axis=0).astype(BF16)


def down(row):
    return jnp.transpose(jnp.broadcast_to(row, (SIDE, SIDE)))


def stencil(lead_row, weight_row):
    f = down(weight_row)
    taps = [
        -f * (f - 1.0) * (f - 2.0) / 6.0,
        (f + 1.0) * (f - 1.0) * (f - 2.0) / 2.0,
        -(f + 1.0) * f * (f - 2.0) / 2.0,
        (f + 1.0) * f * (f - 1.0) / 6.0,
    ]
    distance = iota(SIDE, SIDE, 1).astype(F32) - down(lead_row.astype(F32))
    total = jnp.zeros((SIDE, SIDE), F32)
    for q in range(4):
        total = total + jnp.where(distance == q, taps[q], 0.0)
    return total.astype(BF16)


def kernel(
    groups, members,
    owner_ref, x_hbm, angle_hbm, slope_ref, lead_ref, weight_ref, out_ref,
    x, angle, xs, ys, w1s, w2s, turn, send0, recv0, send1, recv1, lhs, sums, row_tab, chain_rows, chain_ref, tilt_tab, slant_tab, stencils,
    pair_out, pair_in, far_out, far_in, own,
    x_sem, angle_sem, chain_sem, send_sem0, recv_sem0, send_sem1, recv_sem1, pair_send, pair_recv, far_send, far_recv,
):
    layers = groups // 2
    _, sweeps, frequencies = x.shape
    coarse = frequencies // SIDE
    bands = coarse // members
    pieces = send1.shape[1]
    half = bands // pieces
    chunks = sweeps // CHUNK
    angles, all_sweeps = angle.shape
    tilts = angles // SIDE
    sub = lax.axis_index("sub")
    me = lax.axis_index("mem")
    layer, core = sub // 2, sub % 2
    partner = layer * 2 + 1 - core

    barrier = pltpu.get_barrier_semaphore()
    for d in range(1, members):
        pl.semaphore_signal(barrier, inc=1, device_id=(sub, (me + d) % members), device_id_type=MESH)
    pl.semaphore_signal(barrier, inc=1, device_id=(partner, me), device_id_type=MESH)
    for d in range(1, layers):
        other = ((layer + d) % layers) * 2 + core
        pl.semaphore_signal(barrier, inc=1, device_id=(other, me), device_id_type=MESH)

    def x_copy(q):
        rows = pl.ds(pl.multiple_of(q * CHUNK, CHUNK), CHUNK)
        return pltpu.make_async_copy(x_hbm.at[:, rows, :], x.at[:, rows, :], x_sem.at[q])

    for q in range(chunks):
        x_copy(q).start()
    angle_copy = pltpu.make_async_copy(angle_hbm, angle, angle_sem)
    angle_copy.start()

    w1s[...] = stacked_transform(coarse, coarse)
    w2s[...] = stacked_transform(coarse, SIDE)
    c, s = cos_sin((iota(SIDE, SIDE, 0) * iota(SIDE, SIDE, 1)).astype(F32) * (2.0 * math.pi / frequencies))
    turn[0] = c * (1.0 / math.sqrt(frequencies))
    turn[1] = s * (1.0 / math.sqrt(frequencies))

    def mem_copy(h, n, d):
        if h == 1:
            return second_copy(n, d)
        to = (me + d) % members
        return pltpu.make_async_remote_copy(
            src_ref=send0.at[to, n],
            dst_ref=recv0.at[me, n],
            send_sem=send_sem0.at[d - 1, n],
            recv_sem=recv_sem0.at[d - 1, n],
            device_id=(sub, to),
            device_id_type=MESH,
        )

    pl.semaphore_wait(barrier, (members - 1) + 1 + (layers - 1))

    ahead = 1 if chunks > 2 else 0

    def second_copy(n, d):
        to = (me + d) % members
        part = (slice(None), slice(0, ahead)) if n is None else (n, slice(ahead, chunks))
        slot = pieces if n is None else n
        return pltpu.make_async_remote_copy(
            src_ref=send1.at[(to,) + part],
            dst_ref=recv1.at[(me,) + part],
            send_sem=send_sem1.at[d - 1, slot],
            recv_sem=recv_sem1.at[d - 1, slot],
            device_id=(sub, to),
            device_id_type=MESH,
        )

    def transform(q, carry):
        x_copy(q).wait()
        rows = pl.ds(pl.multiple_of(q * CHUNK, CHUNK), CHUNK)

        def spread(k2, inner):
            lanes = pl.ds(pl.multiple_of(k2 * SIDE, SIDE), SIDE)
            for p in range(2):
                at = pl.ds(pl.multiple_of((p * coarse + k2) * CHUNK, CHUNK), CHUNK)
                xs[at, :] = x[p, rows, lanes].astype(F32)
            return inner

        lax.fori_loop(0, coarse, spread, 0, unroll=8)

        batch = CHUNK

        def sweep_batch(step, inner):
            w1 = w1s[...]
            w2 = w2s[...]
            for j in range(0, batch, 2):
                at = [pl.ds(step * batch + j + h, 2 * coarse, stride=CHUNK) for h in range(2)]
                both = jnp.concatenate([xs[at[h], :].astype(BF16) for h in range(2)], axis=1)
                f = jnp.dot(w1, both, preferred_element_type=F32)
                turned = []
                for h in range(2):
                    part = f[:, h * SIDE:(h + 1) * SIDE]
                    re = jnp.concatenate([part[:coarse], part[:coarse]], axis=0)
                    im = jnp.concatenate([part[coarse:], part[coarse:]], axis=0)
                    cosine, sine = turn[0], turn[1]
                    turned.append(jnp.concatenate(
                        [(re * cosine - im * sine).astype(BF16), (re * sine + im * cosine).astype(BF16)], axis=1
                    ))
                y = lax.dot_general(
                    w2, jnp.concatenate(turned, axis=0), (((1,), (1,)), ((), ())), preferred_element_type=F32
                )
                for h in range(2):
                    ys[at[h], :] = y[:, h * SIDE:(h + 1) * SIDE]
            return inner

        lax.fori_loop(0, CHUNK // batch, sweep_batch, 0)

        def pack(band, inner):
            low = iota(CHUNK, SIDE, 1) < SIDE // 2
            piece, local = band // half, band % half
            for m in range(members):
                row = (m * bands + band) * CHUNK
                re = ys[pl.ds(pl.multiple_of(row, CHUNK), CHUNK), :]
                im = ys[pl.ds(pl.multiple_of(coarse * CHUNK + row, CHUNK), CHUNK), :]
                send0[m, q, band] = jnp.where(low, re, pltpu.roll(im, SIDE // 2, 1)).astype(BF16)
                send1[m, piece, q, local] = jnp.where(low, pltpu.roll(re, SIDE // 2, 1), im).astype(BF16)
            return inner

        lax.fori_loop(0, bands, pack, 0, unroll=2)
        for d in range(1, members):
            mem_copy(0, q, d).start()
        return carry

    if ahead:
        lax.fori_loop(0, ahead + 1, transform, 0)
        for d in range(1, members):
            second_copy(None, d).start()
    lax.fori_loop(ahead + 1 if ahead else 0, chunks, transform, 0)
    for piece in range(pieces):
        for d in range(1, members):
            mem_copy(1, piece, d).start()

    angle_copy.wait()
    factor = 1.0 / math.sqrt(all_sweeps)
    for a in range(tilts):
        c, s = cos_sin(angle[a * SIDE:(a + 1) * SIDE, :])
        lhs[a, 0] = (c * factor).astype(BF16)
        lhs[a, 1] = (s * factor).astype(BF16)

    blocks = slope_ref.shape[1]
    row_tab[...] = jnp.zeros_like(row_tab)
    row_tab[0:2, :blocks] = slope_ref[...]
    row_tab[2:3, :blocks] = owner_ref[...].astype(F32)

    def place(block):
        tilt, band = block // bands, block % bands
        return (band // 2) * (2 * tilts) + tilt * 2 + band % 2

    owner_row = row_tab[2:3, :]
    lane = iota(SIDE, SIDE, 1)
    taken = iota(SIDE, SIDE, 0)
    key = jnp.where(lane < blocks, jnp.broadcast_to(owner_row, (SIDE, SIDE)), (lane - blocks).astype(F32))
    limit = jnp.where(lane < blocks, place(lane), blocks)
    earlier = place(taken)
    follows = (key == down(owner_row)) & (taken < blocks) & (earlier < limit)
    chain = jnp.max(jnp.where(follows, earlier + 1, 0), axis=0, keepdims=True)
    chain_rows[...] = jnp.broadcast_to(chain, chain_rows.shape)
    chain_copy = pltpu.make_async_copy(chain_rows, chain_ref, chain_sem)
    chain_copy.start()

    part_lane = iota(SIDE, SIDE, 1)
    sign = jnp.where(part_lane < SIDE // 2, -1.0, 1.0)
    for h in range(2):
        across = (part_lane % (SIDE // 2) + h * (SIDE // 2)).astype(F32)
        c, s = cos_sin(across * down(row_tab[1:2, :]))
        for n, table in enumerate([c, s, sign * c, sign * s]):
            slant_tab[h, n] = table
    c, s = cos_sin(iota(SIDE, SIDE, 0).astype(F32) * row_tab[0:1, :])
    tilt_tab[0] = c
    tilt_tab[1] = s
    for d in range(2):
        stencils[d] = stencil(lead_ref[d:d + 1, :], weight_ref[d:d + 1, :])
    for h in range(2):
        sums[h, 0] = jnp.zeros((SIDE, SIDE), F32)

    recv0[me] = send0[me]
    recv1[me] = send1[me]

    def form(h, piece, i):
        n = piece * (half // 2) + i

        def band_rows(j):
            if h == 0:
                return [recv0[m, q, n * 2 + j] for m in range(members) for q in range(chunks)]
            return [recv1[m, piece, q, i * 2 + j] for m in range(members) for q in range(chunks)]

        rhs = jnp.concatenate([jnp.concatenate(band_rows(j), axis=0) for j in range(2)], axis=1)
        shift = (SIDE - n * 2) % SIDE
        cu = pltpu.roll(tilt_tab[0], shift, 1)
        su = pltpu.roll(tilt_tab[1], shift, 1)
        signs = jnp.where(iota(SIDE, SIDE, 1) < SIDE // 2, -1.0, 1.0)
        for a in range(tilts):
            with_cos = jnp.dot(lhs[a, 0], rhs, preferred_element_type=F32)
            with_sin = jnp.dot(lhs[a, 1], rhs, preferred_element_type=F32)
            for j in range(2):
                b = a * bands + n * 2 + j
                lanes = slice(j * SIDE, (j + 1) * SIDE)
                polar = with_cos[:, lanes] + signs * pltpu.roll(with_sin[:, lanes], SIDE // 2, 1)
                at = a * bands + j
                cb = cu[:, at:at + 1]
                sb = su[:, at:at + 1]
                cv, sv, signed_cv, signed_sv = [slant_tab[h, t, pl.ds(b, 1), :] for t in range(4)]
                cosine = cb * cv - sb * sv
                signed_sine = sb * signed_cv + cb * signed_sv
                demod = polar * cosine + pltpu.roll(polar, SIDE // 2, 1) * signed_sine
                sums[h, n * (2 * tilts) + a * 2 + j + 1] = sums[h, chain_ref[0, b]] + demod

    pairs = half // 2

    def form_piece(h, piece):
        def step(i, carry):
            form(h, piece, i)
            return carry

        lax.fori_loop(0, pairs, step, 0)

    def arrived(q, carry):
        for d in range(1, members):
            mem_copy(0, q, d).wait_recv()
        return carry

    def second_piece(piece, carry):
        for d in range(1, members):
            mem_copy(1, piece, d).wait_recv()
        form_piece(1, piece)
        return carry

    def tile_sum(h, o):
        return sums[h, chain_ref[0, blocks + o]]

    def pair_copy(h, d):
        return pltpu.make_async_remote_copy(
            src_ref=pair_out.at[h, d], dst_ref=pair_in.at[h, d],
            send_sem=pair_send.at[h, d], recv_sem=pair_recv.at[h, d],
            device_id=(partner, me), device_id_type=MESH,
        )

    def far_copy(h, d):
        to = (layer + d) % layers
        return pltpu.make_async_remote_copy(
            src_ref=far_out.at[h, d - 1], dst_ref=far_in.at[h, d - 1],
            send_sem=far_send.at[h, d - 1], recv_sem=far_recv.at[h, d - 1],
            device_id=(to * 2 + core, me), device_id_type=MESH,
        )

    order = list(range(1, layers)) + [0]

    def send_pair(h):
        for d in order:
            pair_out[h, d] = tile_sum(h, ((layer + d) % layers) * 2 + 1 - core).astype(BF16)
            pair_copy(h, d).start()

    def send_far(h):
        for d in range(1, layers):
            mine = tile_sum(h, ((layer + d) % layers) * 2 + core)
            pair_copy(h, d).wait_recv()
            far_out[h, d - 1] = (mine + pair_in[h, d].astype(F32)).astype(BF16)
            far_copy(h, d).start()
        pair_copy(h, 0).wait_recv()
        own[h] = tile_sum(h, layer * 2 + core) + pair_in[h, 0].astype(F32)

    chain_copy.wait()
    lax.fori_loop(0, chunks, arrived, 0)

    def first_step(n, carry):
        form(0, n // pairs, n % pairs)
        return carry

    lax.fori_loop(0, bands // 2, first_step, 0)
    send_pair(0)
    if ahead:
        for d in range(1, members):
            second_copy(None, d).wait_recv()
    second_piece(0, 0)
    send_far(0)
    lax.fori_loop(1, pieces, second_piece, 0)
    send_pair(1)
    send_far(1)
    rows = []
    for h in range(2):
        for d in range(1, layers):
            far_copy(h, d).wait_recv()
            own[h] += far_in[h, d - 1].astype(F32)
        rows.append(jnp.dot(stencils[0], own[h].astype(BF16), preferred_element_type=F32))
    low = iota(SIDE, SIDE, 1) < SIDE // 2
    rows_done = jnp.concatenate(
        [
            jnp.where(low, rows[0], pltpu.roll(rows[1], SIDE // 2, 1)),
            jnp.where(low, pltpu.roll(rows[0], SIDE // 2, 1), rows[1]),
        ],
        axis=0,
    ).astype(BF16)
    tile = lax.dot_general(rows_done, stencils[1], (((1,), (1,)), ((), ())), preferred_element_type=F32)
    out_ref[...] = tile

    if ahead:
        for d in range(1, members):
            second_copy(None, d).wait_send()
    for h, count in ((0, chunks), (1, pieces)):
        def sent(n, carry, h=h):
            for d in range(1, members):
                mem_copy(h, n, d).wait_send()
            return carry

        lax.fori_loop(0, count, sent, 0)
        for d in order:
            pair_copy(h, d).wait_send()
        for d in range(1, layers):
            far_copy(h, d).wait_send()


def on_device(echo, angles, holder, slopes, lead, weight, *, groups, members):
    _, _, sweeps, frequencies = echo.shape
    _, _, angle_count, all_sweeps = angles.shape
    coarse = frequencies // SIDE
    bands = coarse // members
    pieces = min(4, bands // 2)
    half = bands // pieces
    chunks = sweeps // CHUNK
    tilts = angle_count // SIDE
    blocks = slopes.shape[3]
    layers = groups // 2
    exchange0 = (members, chunks, bands, CHUNK, SIDE)
    exchange1 = (members, pieces, chunks, half, CHUNK, SIDE)
    vmem = pl.BlockSpec(memory_space=pltpu.VMEM)
    anywhere = pl.BlockSpec(memory_space=pl.ANY)
    dma = pltpu.SemaphoreType.DMA
    tile = pl.pallas_call(
        functools.partial(kernel, groups, members),
        out_shape=jax.ShapeDtypeStruct((2 * SIDE, SIDE), F32),
        in_specs=[vmem, anywhere, anywhere, vmem, vmem, vmem],
        out_specs=vmem,
        scratch_shapes=[
            pltpu.VMEM((2, sweeps, frequencies), BF16),
            pltpu.VMEM((angle_count, all_sweeps), F32),
            pltpu.VMEM((2 * coarse * CHUNK, SIDE), F32),
            pltpu.VMEM((2 * coarse * CHUNK, SIDE), F32),
            pltpu.VMEM((2 * coarse, 2 * coarse), BF16),
            pltpu.VMEM((2 * coarse, 2 * SIDE), BF16),
            pltpu.VMEM((2, SIDE, SIDE), F32),
            pltpu.VMEM(exchange0, BF16),
            pltpu.VMEM(exchange0, BF16),
            pltpu.VMEM(exchange1, BF16),
            pltpu.VMEM(exchange1, BF16),
            pltpu.VMEM((tilts, 2, SIDE, all_sweeps), BF16),
            pltpu.VMEM((2, blocks + 1, SIDE, SIDE), F32),
            pltpu.VMEM((8, SIDE), F32),
            pltpu.VMEM((8, SIDE), I32),
            pltpu.SMEM((8, SIDE), I32),
            pltpu.VMEM((2, SIDE, SIDE), F32),
            pltpu.VMEM((2, 4, SIDE, SIDE), F32),
            pltpu.VMEM((2, SIDE, SIDE), BF16),
            pltpu.VMEM((2, layers, SIDE, SIDE), BF16),
            pltpu.VMEM((2, layers, SIDE, SIDE), BF16),
            pltpu.VMEM((2, layers - 1, SIDE, SIDE), BF16),
            pltpu.VMEM((2, layers - 1, SIDE, SIDE), BF16),
            pltpu.VMEM((2, SIDE, SIDE), F32),
            dma((chunks,)),
            dma,
            dma,
            dma((members - 1, chunks)),
            dma((members - 1, chunks)),
            dma((members - 1, pieces + 1)),
            dma((members - 1, pieces + 1)),
            dma((2, layers)),
            dma((2, layers)),
            dma((2, layers - 1)),
            dma((2, layers - 1)),
        ],
        compiler_params=pltpu.CompilerParams(
            vmem_limit_bytes=VMEM_LIMIT, collective_id=0, has_side_effects=True
        ),
    )(holder[0], echo[0], angles[0, 0], slopes[0, 0], lead[0, 0], weight[0, 0])
    return (0.25 * tile).astype(BF16).reshape(1, 2, SIDE, SIDE)


def solution(mesh):
    return jax.shard_map(
        functools.partial(on_device, groups=mesh.shape["sub"], members=mesh.shape["mem"]),
        mesh=mesh,
        in_specs=(
            P("sub", None, "mem", None),
            P("sub", "mem", None, None),
            P("sub", "mem", None),
            P("sub", "mem", None, None),
            P("sub", "mem", None, None),
            P("sub", "mem", None, None),
        ),
        out_specs=P(("sub", "mem"), None, None, None),
        check_vma=False,
    )
```

```python
import functools
import math

import jax
import jax.numpy as jnp
from jax import lax
from jax.experimental import pallas as pl
from jax.experimental.pallas import tpu as pltpu
from jax.sharding import PartitionSpec as P

SIDE = 128
CHUNK = 16
F32 = jnp.float32
BF16 = jnp.bfloat16
I32 = jnp.int32
MESH = pl.DeviceIdType.MESH
VMEM_LIMIT = 56 * 1024 * 1024


def cos_sin(x):
    q = jnp.floor(x * (2.0 / math.pi) + 0.5)
    r = x - q * 1.5703125
    r = r - q * 4.837512969970703e-4
    r = r - q * 7.549789948768648e-8
    z = r * r
    s = r + r * z * (-1.6666654611e-1 + z * (8.3321608736e-3 + z * -1.9515295891e-4))
    c = 1.0 - 0.5 * z + z * z * (4.166664568298827e-2 + z * (-1.388731625493765e-3 + z * 2.443315711809948e-5))
    n = q.astype(jnp.int32)
    odd = (n & 1) == 1
    cos_base = jnp.where(odd, s, c)
    sin_base = jnp.where(odd, c, s)
    cos_neg = ((n + 1) & 2) == 2
    sin_neg = (n & 2) == 2
    return jnp.where(cos_neg, -cos_base, cos_base), jnp.where(sin_neg, -sin_base, sin_base)


def iota(rows, columns, dimension):
    return lax.broadcasted_iota(I32, (rows, columns), dimension)


def stacked_transform(coarse, columns):
    turns = (iota(coarse, columns, 0) * iota(coarse, columns, 1)) & (coarse - 1)
    c, s = cos_sin(turns.astype(F32) * (2.0 * math.pi / coarse))
    top = jnp.concatenate([c, -s], axis=1)
    low = jnp.concatenate([s, c], axis=1)
    return jnp.concatenate([top, low], axis=0).astype(BF16)


def down(row):
    return jnp.transpose(jnp.broadcast_to(row, (SIDE, SIDE)))


def stencil(lead_row, weight_row):
    f = down(weight_row)
    taps = [
        -f * (f - 1.0) * (f - 2.0) / 6.0,
        (f + 1.0) * (f - 1.0) * (f - 2.0) / 2.0,
        -(f + 1.0) * f * (f - 2.0) / 2.0,
        (f + 1.0) * f * (f - 1.0) / 6.0,
    ]
    distance = iota(SIDE, SIDE, 1).astype(F32) - down(lead_row.astype(F32))
    total = jnp.zeros((SIDE, SIDE), F32)
    for q in range(4):
        total = total + jnp.where(distance == q, taps[q], 0.0)
    return total.astype(BF16)


def kernel(
    groups, members,
    owner_ref, x_hbm, angle_hbm, slope_ref, lead_ref, weight_ref, out_ref,
    x, angle, xs, ys, w1s, w2s, turn, send0, recv0, send1, recv1, lhs, product, sums, row_tab, chain_rows, chain_ref, tilt_tab, slant_tab, stencils,
    pair_out, pair_in, far_out, far_in, own,
    x_sem, angle_sem, chain_sem, send_sem0, recv_sem0, send_sem1, recv_sem1, pair_send, pair_recv, far_send, far_recv,
):
    layers = groups // 2
    _, sweeps, frequencies = x.shape
    coarse = frequencies // SIDE
    bands = coarse // members
    pieces = send1.shape[1]
    half = bands // pieces
    chunks = sweeps // CHUNK
    angles, all_sweeps = angle.shape
    tilts = angles // SIDE
    sub = lax.axis_index("sub")
    me = lax.axis_index("mem")
    layer, core = sub // 2, sub % 2
    partner = layer * 2 + 1 - core

    barrier = pltpu.get_barrier_semaphore()
    for d in range(1, members):
        pl.semaphore_signal(barrier, inc=1, device_id=(sub, (me + d) % members), device_id_type=MESH)
    pl.semaphore_signal(barrier, inc=1, device_id=(partner, me), device_id_type=MESH)
    for d in range(1, layers):
        other = ((layer + d) % layers) * 2 + core
        pl.semaphore_signal(barrier, inc=1, device_id=(other, me), device_id_type=MESH)

    def x_copy(q):
        rows = pl.ds(pl.multiple_of(q * CHUNK, CHUNK), CHUNK)
        return pltpu.make_async_copy(x_hbm.at[:, rows, :], x.at[:, rows, :], x_sem.at[q])

    for q in range(chunks):
        x_copy(q).start()
    angle_copy = pltpu.make_async_copy(angle_hbm, angle, angle_sem)
    angle_copy.start()

    w1s[...] = stacked_transform(coarse, coarse)
    w2s[...] = stacked_transform(coarse, SIDE)
    c, s = cos_sin((iota(SIDE, SIDE, 0) * iota(SIDE, SIDE, 1)).astype(F32) * (2.0 * math.pi / frequencies))
    turn[0] = c * (1.0 / math.sqrt(frequencies))
    turn[1] = s * (1.0 / math.sqrt(frequencies))

    def mem_copy(h, n, d):
        to = (me + d) % members
        src, dst = ((send0, recv0), (send1, recv1))[h]
        send_sem, recv_sem = ((send_sem0, recv_sem0), (send_sem1, recv_sem1))[h]
        return pltpu.make_async_remote_copy(
            src_ref=src.at[to, n],
            dst_ref=dst.at[me, n],
            send_sem=send_sem.at[d - 1, n],
            recv_sem=recv_sem.at[d - 1, n],
            device_id=(sub, to),
            device_id_type=MESH,
        )

    pl.semaphore_wait(barrier, (members - 1) + 1 + (layers - 1))

    def transform(q, carry):
        x_copy(q).wait()
        rows = pl.ds(pl.multiple_of(q * CHUNK, CHUNK), CHUNK)

        def spread(k2, inner):
            lanes = pl.ds(pl.multiple_of(k2 * SIDE, SIDE), SIDE)
            for p in range(2):
                at = pl.ds(pl.multiple_of((p * coarse + k2) * CHUNK, CHUNK), CHUNK)
                xs[at, :] = x[p, rows, lanes].astype(F32)
            return inner

        lax.fori_loop(0, coarse, spread, 0, unroll=8)

        batch = 8

        def sweep_batch(step, inner):
            w1 = w1s[...]
            w2 = w2s[...]
            for j in range(0, batch, 2):
                at = [pl.ds(step * batch + j + h, 2 * coarse, stride=CHUNK) for h in range(2)]
                both = jnp.concatenate([xs[at[h], :].astype(BF16) for h in range(2)], axis=1)
                f = jnp.dot(w1, both, preferred_element_type=F32)
                turned = []
                for h in range(2):
                    part = f[:, h * SIDE:(h + 1) * SIDE]
                    re = jnp.concatenate([part[:coarse], part[:coarse]], axis=0)
                    im = jnp.concatenate([part[coarse:], part[coarse:]], axis=0)
                    cosine, sine = turn[0], turn[1]
                    turned.append(jnp.concatenate(
                        [(re * cosine - im * sine).astype(BF16), (re * sine + im * cosine).astype(BF16)], axis=1
                    ))
                y = lax.dot_general(
                    w2, jnp.concatenate(turned, axis=0), (((1,), (1,)), ((), ())), preferred_element_type=F32
                )
                for h in range(2):
                    ys[at[h], :] = y[:, h * SIDE:(h + 1) * SIDE]
            return inner

        lax.fori_loop(0, CHUNK // batch, sweep_batch, 0)

        def pack(band, inner):
            low = iota(CHUNK, SIDE, 1) < SIDE // 2
            piece, local = band // half, band % half
            for m in range(members):
                row = (m * bands + band) * CHUNK
                re = ys[pl.ds(pl.multiple_of(row, CHUNK), CHUNK), :]
                im = ys[pl.ds(pl.multiple_of(coarse * CHUNK + row, CHUNK), CHUNK), :]
                send0[m, q, band] = jnp.where(low, re, pltpu.roll(im, SIDE // 2, 1)).astype(BF16)
                send1[m, piece, q, local] = jnp.where(low, pltpu.roll(re, SIDE // 2, 1), im).astype(BF16)
            return inner

        lax.fori_loop(0, bands, pack, 0, unroll=2)
        for d in range(1, members):
            mem_copy(0, q, d).start()
        return carry

    lax.fori_loop(0, chunks, transform, 0)
    for piece in range(pieces):
        for d in range(1, members):
            mem_copy(1, piece, d).start()

    angle_copy.wait()
    factor = 1.0 / math.sqrt(all_sweeps)
    for a in range(tilts):
        c, s = cos_sin(angle[a * SIDE:(a + 1) * SIDE, :])
        lhs[2 * a * SIDE:(2 * a + 1) * SIDE, :] = (c * factor).astype(BF16)
        lhs[(2 * a + 1) * SIDE:(2 * a + 2) * SIDE, :] = (s * factor).astype(BF16)

    blocks = slope_ref.shape[1]
    row_tab[...] = jnp.zeros_like(row_tab)
    row_tab[0:2, :blocks] = slope_ref[...]
    row_tab[2:3, :blocks] = owner_ref[...].astype(F32)

    def place(block):
        tilt, band = block // bands, block % bands
        return (band // 2) * (2 * tilts) + tilt * 2 + band % 2

    owner_row = row_tab[2:3, :]
    lane = iota(SIDE, SIDE, 1)
    taken = iota(SIDE, SIDE, 0)
    key = jnp.where(lane < blocks, jnp.broadcast_to(owner_row, (SIDE, SIDE)), (lane - blocks).astype(F32))
    limit = jnp.where(lane < blocks, place(lane), blocks)
    earlier = place(taken)
    follows = (key == down(owner_row)) & (taken < blocks) & (earlier < limit)
    chain = jnp.max(jnp.where(follows, earlier + 1, 0), axis=0, keepdims=True)
    chain_rows[...] = jnp.broadcast_to(chain, chain_rows.shape)
    chain_copy = pltpu.make_async_copy(chain_rows, chain_ref, chain_sem)
    chain_copy.start()

    part_lane = iota(SIDE, SIDE, 1)
    sign = jnp.where(part_lane < SIDE // 2, -1.0, 1.0)
    for h in range(2):
        across = (part_lane % (SIDE // 2) + h * (SIDE // 2)).astype(F32)
        c, s = cos_sin(across * down(row_tab[1:2, :]))
        for n, table in enumerate([c, s, sign * c, sign * s]):
            slant_tab[h, n] = table
    c, s = cos_sin(iota(SIDE, SIDE, 0).astype(F32) * row_tab[0:1, :])
    tilt_tab[0] = c
    tilt_tab[1] = s
    for d in range(2):
        stencils[d] = stencil(lead_ref[d:d + 1, :], weight_ref[d:d + 1, :])
    for h in range(2):
        sums[h, 0] = jnp.zeros((SIDE, SIDE), F32)

    recv0[me] = send0[me]
    recv1[me] = send1[me]

    def form(h, piece, i):
        n = piece * (half // 2) + i

        def band_rows(j):
            if h == 0:
                return [recv0[m, q, n * 2 + j] for m in range(members) for q in range(chunks)]
            return [recv1[m, piece, q, i * 2 + j] for m in range(members) for q in range(chunks)]

        rhs = jnp.concatenate([jnp.concatenate(band_rows(j), axis=0) for j in range(2)], axis=1)
        shift = (SIDE - n * 2) % SIDE
        cu = pltpu.roll(tilt_tab[0], shift, 1)
        su = pltpu.roll(tilt_tab[1], shift, 1)
        signs = jnp.where(iota(SIDE, SIDE, 1) < SIDE // 2, -1.0, 1.0)
        product[...] = jnp.dot(lhs[...], rhs, preferred_element_type=F32)
        for a in range(tilts):
            for j in range(2):
                b = a * bands + n * 2 + j
                lanes = slice(j * SIDE, (j + 1) * SIDE)
                with_cos = product[2 * a * SIDE:(2 * a + 1) * SIDE, lanes]
                with_sin = product[(2 * a + 1) * SIDE:(2 * a + 2) * SIDE, lanes]
                polar = with_cos + signs * pltpu.roll(with_sin, SIDE // 2, 1)
                at = a * bands + j
                cb = cu[:, at:at + 1]
                sb = su[:, at:at + 1]
                cv, sv, signed_cv, signed_sv = [slant_tab[h, t, pl.ds(b, 1), :] for t in range(4)]
                cosine = cb * cv - sb * sv
                signed_sine = sb * signed_cv + cb * signed_sv
                demod = polar * cosine + pltpu.roll(polar, SIDE // 2, 1) * signed_sine
                sums[h, n * (2 * tilts) + a * 2 + j + 1] = sums[h, chain_ref[0, b]] + demod

    pairs = half // 2

    def form_piece(h, piece):
        def step(i, carry):
            form(h, piece, i)
            return carry

        lax.fori_loop(0, pairs, step, 0)

    def arrived(q, carry):
        for d in range(1, members):
            mem_copy(0, q, d).wait_recv()
        return carry

    def second_piece(piece, carry):
        for d in range(1, members):
            mem_copy(1, piece, d).wait_recv()
        form_piece(1, piece)
        return carry

    def tile_sum(h, o):
        return sums[h, chain_ref[0, blocks + o]]

    def pair_copy(h, d):
        return pltpu.make_async_remote_copy(
            src_ref=pair_out.at[h, d], dst_ref=pair_in.at[h, d],
            send_sem=pair_send.at[h, d], recv_sem=pair_recv.at[h, d],
            device_id=(partner, me), device_id_type=MESH,
        )

    def far_copy(h, d):
        to = (layer + d) % layers
        return pltpu.make_async_remote_copy(
            src_ref=far_out.at[h, d - 1], dst_ref=far_in.at[h, d - 1],
            send_sem=far_send.at[h, d - 1], recv_sem=far_recv.at[h, d - 1],
            device_id=(to * 2 + core, me), device_id_type=MESH,
        )

    order = list(range(1, layers)) + [0]

    def send_pair(h):
        for d in order:
            pair_out[h, d] = tile_sum(h, ((layer + d) % layers) * 2 + 1 - core).astype(BF16)
            pair_copy(h, d).start()

    def send_far(h):
        for d in range(1, layers):
            mine = tile_sum(h, ((layer + d) % layers) * 2 + core)
            pair_copy(h, d).wait_recv()
            far_out[h, d - 1] = (mine + pair_in[h, d].astype(F32)).astype(BF16)
            far_copy(h, d).start()
        pair_copy(h, 0).wait_recv()
        own[h] = tile_sum(h, layer * 2 + core) + pair_in[h, 0].astype(F32)

    chain_copy.wait()
    lax.fori_loop(0, chunks, arrived, 0)

    def first_step(n, carry):
        form(0, n // pairs, n % pairs)
        return carry

    lax.fori_loop(0, bands // 2, first_step, 0)
    send_pair(0)
    second_piece(0, 0)
    send_far(0)
    lax.fori_loop(1, pieces, second_piece, 0)
    send_pair(1)
    send_far(1)
    rows = []
    for h in range(2):
        for d in range(1, layers):
            far_copy(h, d).wait_recv()
            own[h] += far_in[h, d - 1].astype(F32)
        rows.append(jnp.dot(stencils[0], own[h].astype(BF16), preferred_element_type=F32))
    low = iota(SIDE, SIDE, 1) < SIDE // 2
    rows_done = jnp.concatenate(
        [
            jnp.where(low, rows[0], pltpu.roll(rows[1], SIDE // 2, 1)),
            jnp.where(low, pltpu.roll(rows[0], SIDE // 2, 1), rows[1]),
        ],
        axis=0,
    ).astype(BF16)
    tile = lax.dot_general(rows_done, stencils[1], (((1,), (1,)), ((), ())), preferred_element_type=F32)
    out_ref[...] = tile

    for h, count in ((0, chunks), (1, pieces)):
        def sent(n, carry, h=h):
            for d in range(1, members):
                mem_copy(h, n, d).wait_send()
            return carry

        lax.fori_loop(0, count, sent, 0)
        for d in order:
            pair_copy(h, d).wait_send()
        for d in range(1, layers):
            far_copy(h, d).wait_send()


def on_device(echo, angles, holder, slopes, lead, weight, *, groups, members):
    _, _, sweeps, frequencies = echo.shape
    _, _, angle_count, all_sweeps = angles.shape
    coarse = frequencies // SIDE
    bands = coarse // members
    pieces = min(4, bands // 2)
    half = bands // pieces
    chunks = sweeps // CHUNK
    tilts = angle_count // SIDE
    blocks = slopes.shape[3]
    layers = groups // 2
    exchange0 = (members, chunks, bands, CHUNK, SIDE)
    exchange1 = (members, pieces, chunks, half, CHUNK, SIDE)
    vmem = pl.BlockSpec(memory_space=pltpu.VMEM)
    anywhere = pl.BlockSpec(memory_space=pl.ANY)
    dma = pltpu.SemaphoreType.DMA
    tile = pl.pallas_call(
        functools.partial(kernel, groups, members),
        out_shape=jax.ShapeDtypeStruct((2 * SIDE, SIDE), F32),
        in_specs=[vmem, anywhere, anywhere, vmem, vmem, vmem],
        out_specs=vmem,
        scratch_shapes=[
            pltpu.VMEM((2, sweeps, frequencies), BF16),
            pltpu.VMEM((angle_count, all_sweeps), F32),
            pltpu.VMEM((2 * coarse * CHUNK, SIDE), F32),
            pltpu.VMEM((2 * coarse * CHUNK, SIDE), F32),
            pltpu.VMEM((2 * coarse, 2 * coarse), BF16),
            pltpu.VMEM((2 * coarse, 2 * SIDE), BF16),
            pltpu.VMEM((2, SIDE, SIDE), F32),
            pltpu.VMEM(exchange0, BF16),
            pltpu.VMEM(exchange0, BF16),
            pltpu.VMEM(exchange1, BF16),
            pltpu.VMEM(exchange1, BF16),
            pltpu.VMEM((2 * angle_count, all_sweeps), BF16),
            pltpu.VMEM((2 * angle_count, 2 * SIDE), F32),
            pltpu.VMEM((2, blocks + 1, SIDE, SIDE), F32),
            pltpu.VMEM((8, SIDE), F32),
            pltpu.VMEM((8, SIDE), I32),
            pltpu.SMEM((8, SIDE), I32),
            pltpu.VMEM((2, SIDE, SIDE), F32),
            pltpu.VMEM((2, 4, SIDE, SIDE), F32),
            pltpu.VMEM((2, SIDE, SIDE), BF16),
            pltpu.VMEM((2, layers, SIDE, SIDE), BF16),
            pltpu.VMEM((2, layers, SIDE, SIDE), BF16),
            pltpu.VMEM((2, layers - 1, SIDE, SIDE), BF16),
            pltpu.VMEM((2, layers - 1, SIDE, SIDE), BF16),
            pltpu.VMEM((2, SIDE, SIDE), F32),
            dma((chunks,)),
            dma,
            dma,
            dma((members - 1, chunks)),
            dma((members - 1, chunks)),
            dma((members - 1, pieces)),
            dma((members - 1, pieces)),
            dma((2, layers)),
            dma((2, layers)),
            dma((2, layers - 1)),
            dma((2, layers - 1)),
        ],
        compiler_params=pltpu.CompilerParams(
            vmem_limit_bytes=VMEM_LIMIT, collective_id=0, has_side_effects=True
        ),
    )(holder[0], echo[0], angles[0, 0], slopes[0, 0], lead[0, 0], weight[0, 0])
    return (0.25 * tile).astype(BF16).reshape(1, 2, SIDE, SIDE)


def solution(mesh):
    return jax.shard_map(
        functools.partial(on_device, groups=mesh.shape["sub"], members=mesh.shape["mem"]),
        mesh=mesh,
        in_specs=(
            P("sub", None, "mem", None),
            P("sub", "mem", None, None),
            P("sub", "mem", None),
            P("sub", "mem", None, None),
            P("sub", "mem", None, None),
            P("sub", "mem", None, None),
        ),
        out_specs=P(("sub", "mem"), None, None, None),
        check_vma=False,
    )
```

```python
import functools
import math

import jax
import jax.numpy as jnp
from jax import lax
from jax.experimental import pallas as pl
from jax.experimental.pallas import tpu as pltpu
from jax.sharding import PartitionSpec as P

SIDE = 128
CHUNK = 16
F32 = jnp.float32
BF16 = jnp.bfloat16
I32 = jnp.int32
MESH = pl.DeviceIdType.MESH
VMEM_LIMIT = 56 * 1024 * 1024


def cos_sin(x):
    q = jnp.floor(x * (2.0 / math.pi) + 0.5)
    r = x - q * 1.5703125
    r = r - q * 4.837512969970703e-4
    r = r - q * 7.549789948768648e-8
    z = r * r
    s = r + r * z * (-1.6666654611e-1 + z * (8.3321608736e-3 + z * -1.9515295891e-4))
    c = 1.0 - 0.5 * z + z * z * (4.166664568298827e-2 + z * (-1.388731625493765e-3 + z * 2.443315711809948e-5))
    n = q.astype(jnp.int32)
    odd = (n & 1) == 1
    cos_base = jnp.where(odd, s, c)
    sin_base = jnp.where(odd, c, s)
    cos_neg = ((n + 1) & 2) == 2
    sin_neg = (n & 2) == 2
    return jnp.where(cos_neg, -cos_base, cos_base), jnp.where(sin_neg, -sin_base, sin_base)


def iota(rows, columns, dimension):
    return lax.broadcasted_iota(I32, (rows, columns), dimension)


def stacked_transform(coarse, columns):
    turns = (iota(coarse, columns, 0) * iota(coarse, columns, 1)) & (coarse - 1)
    c, s = cos_sin(turns.astype(F32) * (2.0 * math.pi / coarse))
    top = jnp.concatenate([c, -s], axis=1)
    low = jnp.concatenate([s, c], axis=1)
    return jnp.concatenate([top, low], axis=0).astype(BF16)


def down(row):
    return jnp.transpose(jnp.broadcast_to(row, (SIDE, SIDE)))


def stencil(lead_row, weight_row):
    f = down(weight_row)
    taps = [
        -f * (f - 1.0) * (f - 2.0) / 6.0,
        (f + 1.0) * (f - 1.0) * (f - 2.0) / 2.0,
        -(f + 1.0) * f * (f - 2.0) / 2.0,
        (f + 1.0) * f * (f - 1.0) / 6.0,
    ]
    distance = iota(SIDE, SIDE, 1).astype(F32) - down(lead_row.astype(F32))
    total = jnp.zeros((SIDE, SIDE), F32)
    for q in range(4):
        total = total + jnp.where(distance == q, taps[q], 0.0)
    return total.astype(BF16)


def kernel(
    groups, members,
    owner_ref, x_hbm, angle_hbm, slope_ref, lead_ref, weight_ref, out_ref,
    x, angle, xs, ys, w1s, w2s, turn, send0, recv0, send1, recv1, lhs, product, sums, row_tab, chain_rows, chain_ref, tilt_tab, slant_tab, stencils,
    pair_out, pair_in, far_out, far_in, own,
    x_sem, angle_sem, chain_sem, send_sem0, recv_sem0, send_sem1, recv_sem1, pair_send, pair_recv, far_send, far_recv,
):
    layers = groups // 2
    _, sweeps, frequencies = x.shape
    coarse = frequencies // SIDE
    bands = coarse // members
    pieces = send1.shape[1]
    half = bands // pieces
    chunks = sweeps // CHUNK
    angles, all_sweeps = angle.shape
    tilts = angles // SIDE
    sub = lax.axis_index("sub")
    me = lax.axis_index("mem")
    layer, core = sub // 2, sub % 2
    partner = layer * 2 + 1 - core

    barrier = pltpu.get_barrier_semaphore()
    for d in range(1, members):
        pl.semaphore_signal(barrier, inc=1, device_id=(sub, (me + d) % members), device_id_type=MESH)
    pl.semaphore_signal(barrier, inc=1, device_id=(partner, me), device_id_type=MESH)
    for d in range(1, layers):
        other = ((layer + d) % layers) * 2 + core
        pl.semaphore_signal(barrier, inc=1, device_id=(other, me), device_id_type=MESH)

    def x_copy(q):
        rows = pl.ds(pl.multiple_of(q * CHUNK, CHUNK), CHUNK)
        return pltpu.make_async_copy(x_hbm.at[:, rows, :], x.at[:, rows, :], x_sem.at[q])

    for q in range(chunks):
        x_copy(q).start()
    angle_copy = pltpu.make_async_copy(angle_hbm, angle, angle_sem)
    angle_copy.start()

    w1s[...] = stacked_transform(coarse, coarse)
    w2s[...] = stacked_transform(coarse, SIDE)
    c, s = cos_sin((iota(SIDE, SIDE, 0) * iota(SIDE, SIDE, 1)).astype(F32) * (2.0 * math.pi / frequencies))
    turn[0] = c * (1.0 / math.sqrt(frequencies))
    turn[1] = s * (1.0 / math.sqrt(frequencies))

    def mem_copy(h, n, d):
        to = (me + d) % members
        src, dst = ((send0, recv0), (send1, recv1))[h]
        send_sem, recv_sem = ((send_sem0, recv_sem0), (send_sem1, recv_sem1))[h]
        return pltpu.make_async_remote_copy(
            src_ref=src.at[to, n],
            dst_ref=dst.at[me, n],
            send_sem=send_sem.at[d - 1, n],
            recv_sem=recv_sem.at[d - 1, n],
            device_id=(sub, to),
            device_id_type=MESH,
        )

    pl.semaphore_wait(barrier, (members - 1) + 1 + (layers - 1))

    def transform(q, carry):
        x_copy(q).wait()
        rows = pl.ds(pl.multiple_of(q * CHUNK, CHUNK), CHUNK)

        def spread(k2, inner):
            lanes = pl.ds(pl.multiple_of(k2 * SIDE, SIDE), SIDE)
            for p in range(2):
                at = pl.ds(pl.multiple_of((p * coarse + k2) * CHUNK, CHUNK), CHUNK)
                xs[at, :] = x[p, rows, lanes].astype(F32)
            return inner

        lax.fori_loop(0, coarse, spread, 0, unroll=8)

        batch = 4

        def sweep_batch(step, inner):
            w1 = w1s[...]
            w2 = w2s[...]
            for j in range(0, batch, 2):
                at = [pl.ds(step * batch + j + h, 2 * coarse, stride=CHUNK) for h in range(2)]
                both = jnp.concatenate([xs[at[h], :].astype(BF16) for h in range(2)], axis=1)
                f = jnp.dot(w1, both, preferred_element_type=F32)
                turned = []
                for h in range(2):
                    part = f[:, h * SIDE:(h + 1) * SIDE]
                    re = jnp.concatenate([part[:coarse], part[:coarse]], axis=0)
                    im = jnp.concatenate([part[coarse:], part[coarse:]], axis=0)
                    cosine, sine = turn[0], turn[1]
                    turned.append(jnp.concatenate(
                        [(re * cosine - im * sine).astype(BF16), (re * sine + im * cosine).astype(BF16)], axis=1
                    ))
                y = lax.dot_general(
                    w2, jnp.concatenate(turned, axis=0), (((1,), (1,)), ((), ())), preferred_element_type=F32
                )
                for h in range(2):
                    ys[at[h], :] = y[:, h * SIDE:(h + 1) * SIDE]
            return inner

        lax.fori_loop(0, CHUNK // batch, sweep_batch, 0)

        def pack(band, inner):
            low = iota(CHUNK, SIDE, 1) < SIDE // 2
            piece, local = band // half, band % half
            for m in range(members):
                row = (m * bands + band) * CHUNK
                re = ys[pl.ds(pl.multiple_of(row, CHUNK), CHUNK), :]
                im = ys[pl.ds(pl.multiple_of(coarse * CHUNK + row, CHUNK), CHUNK), :]
                send0[m, q, band] = jnp.where(low, re, pltpu.roll(im, SIDE // 2, 1)).astype(BF16)
                send1[m, piece, q, local] = jnp.where(low, pltpu.roll(re, SIDE // 2, 1), im).astype(BF16)
            return inner

        lax.fori_loop(0, bands, pack, 0, unroll=2)
        for d in range(1, members):
            mem_copy(0, q, d).start()
        return carry

    lax.fori_loop(0, chunks, transform, 0)
    for piece in range(pieces):
        for d in range(1, members):
            mem_copy(1, piece, d).start()

    angle_copy.wait()
    factor = 1.0 / math.sqrt(all_sweeps)
    for a in range(tilts):
        c, s = cos_sin(angle[a * SIDE:(a + 1) * SIDE, :])
        lhs[2 * a * SIDE:(2 * a + 1) * SIDE, :] = (c * factor).astype(BF16)
        lhs[(2 * a + 1) * SIDE:(2 * a + 2) * SIDE, :] = (s * factor).astype(BF16)

    blocks = slope_ref.shape[1]
    row_tab[...] = jnp.zeros_like(row_tab)
    row_tab[0:2, :blocks] = slope_ref[...]
    row_tab[2:3, :blocks] = owner_ref[...].astype(F32)

    def place(block):
        tilt, band = block // bands, block % bands
        return (band // 2) * (2 * tilts) + tilt * 2 + band % 2

    owner_row = row_tab[2:3, :]
    lane = iota(SIDE, SIDE, 1)
    taken = iota(SIDE, SIDE, 0)
    key = jnp.where(lane < blocks, jnp.broadcast_to(owner_row, (SIDE, SIDE)), (lane - blocks).astype(F32))
    limit = jnp.where(lane < blocks, place(lane), blocks)
    earlier = place(taken)
    follows = (key == down(owner_row)) & (taken < blocks) & (earlier < limit)
    chain = jnp.max(jnp.where(follows, earlier + 1, 0), axis=0, keepdims=True)
    chain_rows[...] = jnp.broadcast_to(chain, chain_rows.shape)
    chain_copy = pltpu.make_async_copy(chain_rows, chain_ref, chain_sem)
    chain_copy.start()

    part_lane = iota(SIDE, SIDE, 1)
    sign = jnp.where(part_lane < SIDE // 2, -1.0, 1.0)
    for h in range(2):
        across = (part_lane % (SIDE // 2) + h * (SIDE // 2)).astype(F32)
        c, s = cos_sin(across * down(row_tab[1:2, :]))
        for n, table in enumerate([c, s, sign * c, sign * s]):
            slant_tab[h, n] = table
    c, s = cos_sin(iota(SIDE, SIDE, 0).astype(F32) * row_tab[0:1, :])
    tilt_tab[0] = c
    tilt_tab[1] = s
    for d in range(2):
        stencils[d] = stencil(lead_ref[d:d + 1, :], weight_ref[d:d + 1, :])
    for h in range(2):
        sums[h, 0] = jnp.zeros((SIDE, SIDE), F32)

    recv0[me] = send0[me]
    recv1[me] = send1[me]

    def form(h, piece, i):
        n = piece * (half // 2) + i

        def band_rows(j):
            if h == 0:
                return [recv0[m, q, n * 2 + j] for m in range(members) for q in range(chunks)]
            return [recv1[m, piece, q, i * 2 + j] for m in range(members) for q in range(chunks)]

        rhs = jnp.concatenate([jnp.concatenate(band_rows(j), axis=0) for j in range(2)], axis=1)
        shift = (SIDE - n * 2) % SIDE
        cu = pltpu.roll(tilt_tab[0], shift, 1)
        su = pltpu.roll(tilt_tab[1], shift, 1)
        signs = jnp.where(iota(SIDE, SIDE, 1) < SIDE // 2, -1.0, 1.0)
        product[...] = jnp.dot(lhs[...], rhs, preferred_element_type=F32)
        for a in range(tilts):
            for j in range(2):
                b = a * bands + n * 2 + j
                lanes = slice(j * SIDE, (j + 1) * SIDE)
                with_cos = product[2 * a * SIDE:(2 * a + 1) * SIDE, lanes]
                with_sin = product[(2 * a + 1) * SIDE:(2 * a + 2) * SIDE, lanes]
                polar = with_cos + signs * pltpu.roll(with_sin, SIDE // 2, 1)
                at = a * bands + j
                cb = cu[:, at:at + 1]
                sb = su[:, at:at + 1]
                cv, sv, signed_cv, signed_sv = [slant_tab[h, t, pl.ds(b, 1), :] for t in range(4)]
                cosine = cb * cv - sb * sv
                signed_sine = sb * signed_cv + cb * signed_sv
                demod = polar * cosine + pltpu.roll(polar, SIDE // 2, 1) * signed_sine
                sums[h, n * (2 * tilts) + a * 2 + j + 1] = sums[h, chain_ref[0, b]] + demod

    pairs = half // 2

    def form_piece(h, piece):
        def step(i, carry):
            form(h, piece, i)
            return carry

        lax.fori_loop(0, pairs, step, 0)

    def arrived(q, carry):
        for d in range(1, members):
            mem_copy(0, q, d).wait_recv()
        return carry

    def second_piece(piece, carry):
        for d in range(1, members):
            mem_copy(1, piece, d).wait_recv()
        form_piece(1, piece)
        return carry

    def tile_sum(h, o):
        return sums[h, chain_ref[0, blocks + o]]

    def pair_copy(h, d):
        return pltpu.make_async_remote_copy(
            src_ref=pair_out.at[h, d], dst_ref=pair_in.at[h, d],
            send_sem=pair_send.at[h, d], recv_sem=pair_recv.at[h, d],
            device_id=(partner, me), device_id_type=MESH,
        )

    def far_copy(h, d):
        to = (layer + d) % layers
        return pltpu.make_async_remote_copy(
            src_ref=far_out.at[h, d - 1], dst_ref=far_in.at[h, d - 1],
            send_sem=far_send.at[h, d - 1], recv_sem=far_recv.at[h, d - 1],
            device_id=(to * 2 + core, me), device_id_type=MESH,
        )

    order = list(range(1, layers)) + [0]

    def send_pair(h):
        for d in order:
            pair_out[h, d] = tile_sum(h, ((layer + d) % layers) * 2 + 1 - core).astype(BF16)
            pair_copy(h, d).start()

    def send_far(h):
        for d in range(1, layers):
            mine = tile_sum(h, ((layer + d) % layers) * 2 + core)
            pair_copy(h, d).wait_recv()
            far_out[h, d - 1] = (mine + pair_in[h, d].astype(F32)).astype(BF16)
            far_copy(h, d).start()
        pair_copy(h, 0).wait_recv()
        own[h] = tile_sum(h, layer * 2 + core) + pair_in[h, 0].astype(F32)

    chain_copy.wait()
    lax.fori_loop(0, chunks, arrived, 0)

    def first_step(n, carry):
        form(0, n // pairs, n % pairs)
        return carry

    lax.fori_loop(0, bands // 2, first_step, 0)
    send_pair(0)
    second_piece(0, 0)
    send_far(0)
    lax.fori_loop(1, pieces, second_piece, 0)
    send_pair(1)
    send_far(1)
    rows = []
    for h in range(2):
        for d in range(1, layers):
            far_copy(h, d).wait_recv()
            own[h] += far_in[h, d - 1].astype(F32)
        rows.append(jnp.dot(stencils[0], own[h].astype(BF16), preferred_element_type=F32))
    low = iota(SIDE, SIDE, 1) < SIDE // 2
    rows_done = jnp.concatenate(
        [
            jnp.where(low, rows[0], pltpu.roll(rows[1], SIDE // 2, 1)),
            jnp.where(low, pltpu.roll(rows[0], SIDE // 2, 1), rows[1]),
        ],
        axis=0,
    ).astype(BF16)
    tile = lax.dot_general(rows_done, stencils[1], (((1,), (1,)), ((), ())), preferred_element_type=F32)
    out_ref[...] = tile

    for h, count in ((0, chunks), (1, pieces)):
        def sent(n, carry, h=h):
            for d in range(1, members):
                mem_copy(h, n, d).wait_send()
            return carry

        lax.fori_loop(0, count, sent, 0)
        for d in order:
            pair_copy(h, d).wait_send()
        for d in range(1, layers):
            far_copy(h, d).wait_send()


def on_device(echo, angles, holder, slopes, lead, weight, *, groups, members):
    _, _, sweeps, frequencies = echo.shape
    _, _, angle_count, all_sweeps = angles.shape
    coarse = frequencies // SIDE
    bands = coarse // members
    pieces = min(4, bands // 2)
    half = bands // pieces
    chunks = sweeps // CHUNK
    tilts = angle_count // SIDE
    blocks = slopes.shape[3]
    layers = groups // 2
    exchange0 = (members, chunks, bands, CHUNK, SIDE)
    exchange1 = (members, pieces, chunks, half, CHUNK, SIDE)
    vmem = pl.BlockSpec(memory_space=pltpu.VMEM)
    anywhere = pl.BlockSpec(memory_space=pl.ANY)
    dma = pltpu.SemaphoreType.DMA
    tile = pl.pallas_call(
        functools.partial(kernel, groups, members),
        out_shape=jax.ShapeDtypeStruct((2 * SIDE, SIDE), F32),
        in_specs=[vmem, anywhere, anywhere, vmem, vmem, vmem],
        out_specs=vmem,
        scratch_shapes=[
            pltpu.VMEM((2, sweeps, frequencies), BF16),
            pltpu.VMEM((angle_count, all_sweeps), F32),
            pltpu.VMEM(((2 * coarse + 1) * CHUNK, SIDE), F32),
            pltpu.VMEM(((2 * coarse + 1) * CHUNK, SIDE), F32),
            pltpu.VMEM((2 * coarse, 2 * coarse), BF16),
            pltpu.VMEM((2 * coarse, 2 * SIDE), BF16),
            pltpu.VMEM((2, SIDE, SIDE), F32),
            pltpu.VMEM(exchange0, BF16),
            pltpu.VMEM(exchange0, BF16),
            pltpu.VMEM(exchange1, BF16),
            pltpu.VMEM(exchange1, BF16),
            pltpu.VMEM((2 * angle_count, all_sweeps), BF16),
            pltpu.VMEM((2 * angle_count, 2 * SIDE), F32),
            pltpu.VMEM((2, blocks + 1, SIDE, SIDE), F32),
            pltpu.VMEM((8, SIDE), F32),
            pltpu.VMEM((8, SIDE), I32),
            pltpu.SMEM((8, SIDE), I32),
            pltpu.VMEM((2, SIDE, SIDE), F32),
            pltpu.VMEM((2, 4, SIDE, SIDE), F32),
            pltpu.VMEM((2, SIDE, SIDE), BF16),
            pltpu.VMEM((2, layers, SIDE, SIDE), BF16),
            pltpu.VMEM((2, layers, SIDE, SIDE), BF16),
            pltpu.VMEM((2, layers - 1, SIDE, SIDE), BF16),
            pltpu.VMEM((2, layers - 1, SIDE, SIDE), BF16),
            pltpu.VMEM((2, SIDE, SIDE), F32),
            dma((chunks,)),
            dma,
            dma,
            dma((members - 1, chunks)),
            dma((members - 1, chunks)),
            dma((members - 1, pieces)),
            dma((members - 1, pieces)),
            dma((2, layers)),
            dma((2, layers)),
            dma((2, layers - 1)),
            dma((2, layers - 1)),
        ],
        compiler_params=pltpu.CompilerParams(
            vmem_limit_bytes=VMEM_LIMIT, collective_id=0, has_side_effects=True
        ),
    )(holder[0], echo[0], angles[0, 0], slopes[0, 0], lead[0, 0], weight[0, 0])
    return (0.25 * tile).astype(BF16).reshape(1, 2, SIDE, SIDE)


def solution(mesh):
    return jax.shard_map(
        functools.partial(on_device, groups=mesh.shape["sub"], members=mesh.shape["mem"]),
        mesh=mesh,
        in_specs=(
            P("sub", None, "mem", None),
            P("sub", "mem", None, None),
            P("sub", "mem", None),
            P("sub", "mem", None, None),
            P("sub", "mem", None, None),
            P("sub", "mem", None, None),
        ),
        out_specs=P(("sub", "mem"), None, None, None),
        check_vma=False,
    )
```
